32 devices in a mesh: dp: 8 (over y, x, core), seq: 4 (over z).
Axes of the slice: x: 2, y: 2, z: 4, core: 2. Of those that a mesh axis runs over, the one named last changes fastest.
Arguments:
- tokens: bfloat16 [8, 1024, 5120], P('dp', 'seq'), may hold values from -6 to 6
- queries: bfloat16 [8, 1024, 2560], P('dp', 'seq'), may hold values from -400 to 400
- cotangent: bfloat16 [8, 1024, 2560], P('dp', 'seq'), may hold values from -6 to 6
- kv_weight: bfloat16 [5120, 1024], P('dp'), may hold values from -0.078125 to 0.078125
- active: int32 [8, 4], P('dp'), may hold values from 0 to 7, as said below
Outputs:
- query_grads: bfloat16 [8, 1024, 2560], P('dp', 'seq')
- token_grads: bfloat16 [8, 1024, 5120], P('dp', 'seq')
- weight_grad: float32 [5120, 1024], P('dp', 'seq')
The draws below stay inside these ranges and needn't reach their ends.
Inputs may be any that keep to these rules, and one draw needn't show every extreme that they name: active[p] lists 4 different blocks of sequence p in increasing order; blocks 0 and 7 are always among them.
All inputs are finite; a program needn't handle non-finite values.
Results may differ from the reference program's by a relative error of at most 0.019.
The reference program's roundings to bfloat16 on the way count: a program that leaves them out, or rounds other values in their place, can miss the bound.
Values may be sent and summed in bfloat16 or wider, within the bound.
No kernel may reach another device: no remote copies, remote signals or barrier semaphores. Data moves between devices by JAX's collectives and lax.ppermute only.
A program may use at most 128 MiB of HBM per device.

```python
import math
import jax
import jax.numpy as jnp
from jax import lax

D = 5120
HEAD_SIZE = 128
QUERY_HEADS = 20
KEY_VALUE_HEADS = 4
BLK = 128
TOK_DEV = 256
SEQLEN = 1024
NBLK = 8
NACT = 4
QW = 2560
KVW = 1024
N_DP = 8
N_SEQ = 4


def draw_queries(key, part):
    key_base, key_scale = jax.random.split(key)
    base = jax.random.normal(key_base, (N_DP, SEQLEN, QUERY_HEADS * HEAD_SIZE), jnp.float32)
    spread_log = jax.random.uniform(key_scale, (N_DP, SEQLEN, 1), jnp.float32, math.log(0.5), math.log(2.0))
    return jnp.clip(base * jnp.exp(spread_log), -400.0, 400.0).astype(jnp.bfloat16)


def draw_active(key, part):

    def one_row(row_key):
        inner = jax.random.permutation(row_key, NBLK - 2)[:NACT - 2] + 1
        chosen = jnp.concatenate([jnp.zeros((1,), jnp.int32), inner.astype(jnp.int32), jnp.full((1,), NBLK - 1, jnp.int32)])
        return jnp.sort(chosen)
    return jax.vmap(one_row)(jax.random.split(key, N_DP))


def level_of(key, shape, shards, smallest, top_value):
    factor_of, own = 1.0, jax.random.fold_in(key, 6)
    for axis_at, parts in shards:
        heights = jnp.exp(jax.random.uniform(jax.random.fold_in(own, axis_at), (parts,), jnp.float32, smallest / len(shards), top_value / len(shards)))
        factor_of = factor_of * jnp.repeat(heights, shape[axis_at] // parts).reshape([-1 if axis == axis_at else 1 for axis in range(len(shape))])
    return factor_of


def scatter_about(key, dims, deviation, limit, cuts=(), kind=jnp.bfloat16):
    gain = level_of(key, dims, cuts, -0.22, 0.18) if cuts else 1.0
    drawn = jax.random.normal(key, dims, jnp.float32) * deviation * gain
    return jnp.minimum(jnp.maximum(drawn, -limit), limit).astype(kind)


def setup_inputs(seed: int = 0) -> dict:
    key_of = jax.random.split(jax.random.key(seed), 6)
    return {
        "tokens": scatter_about(key_of[0], (N_DP, SEQLEN, D), 1.0, 6.0, ((0, 8), (1, 4))),
        "queries": draw_queries(jax.random.fold_in(key_of[5], 71), 0),
        "cotangent": scatter_about(key_of[2], (N_DP, SEQLEN, QW), 1.0, 6.0, ((0, 8), (1, 4))),
        "kv_weight": scatter_about(key_of[3], (D, KVW), D ** -0.5, 0.078125, ((0, 8),)),
        "active": draw_active(jax.random.fold_in(key_of[5], 71), 0),
    }


def lower_precision(value):
    return lax.optimization_barrier(value.astype(jnp.bfloat16))

def reference(tokens, queries, cotangent, kv_weight, active):
    head_group = QUERY_HEADS // KEY_VALUE_HEADS
    routed_count = NACT * BLK
    scale = 1.0 / math.sqrt(HEAD_SIZE)

    def one_sequence(grad_total, pieces):
        tokens_p, query_parts, output_cotangent_parts, block_ids = pieces
        token_positions = (block_ids[:, None] * BLK + jnp.arange(BLK, dtype=jnp.int32)[None, :]).reshape(-1).astype(jnp.int32)
        x_act = tokens_p[token_positions]
        keyval = lower_precision(jnp.dot(x_act, kv_weight, preferred_element_type=jnp.float32))
        key_value_wide = keyval.astype(jnp.float32)
        key_matrix = key_value_wide[:, :KEY_VALUE_HEADS * HEAD_SIZE].reshape(routed_count, KEY_VALUE_HEADS, HEAD_SIZE)
        value_matrix = key_value_wide[:, KEY_VALUE_HEADS * HEAD_SIZE:].reshape(routed_count, KEY_VALUE_HEADS, HEAD_SIZE)
        active_query = query_parts[token_positions].astype(jnp.float32).reshape(routed_count, KEY_VALUE_HEADS, head_group, HEAD_SIZE)
        active_gradient = output_cotangent_parts[token_positions].astype(jnp.float32).reshape(routed_count, KEY_VALUE_HEADS, head_group, HEAD_SIZE)
        scores = jnp.einsum('ikgd,jkd->kgij', active_query, key_matrix) * scale
        causal = jnp.arange(routed_count)[None, :] <= jnp.arange(routed_count)[:, None]
        scores = jnp.where(causal, scores, -1e+30)
        row_max = lax.optimization_barrier(jnp.max(scores, axis=-1, keepdims=True))
        exponent = jnp.exp(scores - row_max)
        probs = exponent / lax.optimization_barrier(jnp.sum(exponent, axis=-1, keepdims=True))
        probs_low = lower_precision(probs).astype(jnp.float32)
        attended = jnp.einsum('kgij,jkd->ikgd', probs_low, value_matrix)
        row_delta = jnp.einsum('ikgd,ikgd->kgi', active_gradient, attended)
        dprobs = jnp.einsum('ikgd,jkd->kgij', active_gradient, value_matrix)
        dscores = lower_precision(probs * (dprobs - row_delta[..., None]) * scale).astype(jnp.float32)
        query_grad = jnp.einsum('kgij,jkd->ikgd', dscores, key_matrix).astype(jnp.bfloat16).reshape(routed_count, QW)
        key_gradient = jnp.einsum('kgij,ikgd->jkd', dscores, active_query)
        value_gradient = jnp.einsum('kgij,ikgd->jkd', probs_low, active_gradient)
        key_value_gradient = lower_precision(jnp.concatenate([key_gradient.reshape(routed_count, KEY_VALUE_HEADS * HEAD_SIZE), value_gradient.reshape(routed_count, KEY_VALUE_HEADS * HEAD_SIZE)], axis=1))
        token_grad = lax.dot_general(key_value_gradient, kv_weight, (((1,), (1,)), ((), ())), preferred_element_type=jnp.float32).astype(jnp.bfloat16)
        full_query = jnp.zeros((SEQLEN, QW), jnp.bfloat16).at[token_positions].set(query_grad)
        full_token = jnp.zeros((SEQLEN, D), jnp.bfloat16).at[token_positions].set(token_grad)
        full_kv = jnp.zeros((SEQLEN, KVW), jnp.bfloat16).at[token_positions].set(key_value_gradient)
        terms = jnp.einsum('std,stc->sdc', tokens_p.reshape(N_SEQ, TOK_DEV, D).astype(jnp.float32), full_kv.reshape(N_SEQ, TOK_DEV, KVW).astype(jnp.float32))
        grad_total = grad_total + lax.optimization_barrier(jnp.sum(lower_precision(terms).astype(jnp.float32), axis=0))
        return (grad_total, (full_query, full_token))
    weight_grad, outputs = lax.scan(one_sequence, jnp.zeros((D, KVW), jnp.float32), (tokens, queries, cotangent, active))
    return (outputs[0], outputs[1], weight_grad)
```

```python
import functools
import math

import jax
import jax.numpy as jnp
from jax import lax
from jax.experimental import pallas as pl
from jax.experimental.pallas import tpu as pltpu
from jax.sharding import PartitionSpec as P

HEAD_SIZE = 128
BLK = 128
CHUNKS = 2
VMEM_BYTES = 48 * 1024 * 1024
MASKED = -1e30


def params():
    return pltpu.CompilerParams(vmem_limit_bytes=VMEM_BYTES)


def vmem():
    return pl.BlockSpec(memory_space=pltpu.VMEM)


def smem():
    return pl.BlockSpec(memory_space=pltpu.SMEM)


def dot(left, right, left_dim, right_dim):
    return lax.dot_general(
        left, right, (((left_dim,), (right_dim,)), ((), ())), preferred_element_type=jnp.float32
    )


def exchange(value, axis, mask):
    count = lax.axis_size(axis)
    return lax.ppermute(value, axis, [(i, i ^ mask) for i in range(count)])


def moved(value, axis, step):
    count = lax.axis_size(axis)
    pairs = [(i, i + step) for i in range(count) if 0 <= i + step < count]
    return lax.ppermute(value, axis, pairs)


def half(piece, side):
    if len(piece) == 2:
        return piece[side]
    width = piece[0].shape[1] // 2
    return piece[0][:, side * width : (side + 1) * width]


def gather_pieces(own):
    count = lax.axis_size("dp")
    pieces = {0: (own,)}
    for mask in sorted(range(2, count, 2), key=lambda m: (m.bit_count(), m)):
        low, high = mask & -mask, 1 << (mask.bit_length() - 1)
        if low == high:
            pieces[mask] = (exchange(own, "dp", mask),)
        else:
            pieces[mask] = (
                exchange(half(pieces[mask ^ high], 0), "dp", high),
                exchange(half(pieces[mask ^ low], 1), "dp", low),
            )
    for mask in list(pieces):
        pieces[mask | 1] = tuple(exchange(part, "dp", 1) for part in pieces[mask])
    return [pieces[mask] for mask in range(count)]


def unflatten(lengths, refs):
    grouped, at = [], 0
    for length in lengths:
        grouped.append(refs[at : at + length])
        at += length
    return grouped


def side_of(piece, side):
    if len(piece) == 2:
        return piece[side][...]
    width = piece[0].shape[1] // 2
    return piece[0][:, side * width : (side + 1) * width]


def project_kernel(lengths, x_ref, *refs):
    out_ref = refs[-1]
    pieces = unflatten(lengths, refs[:-1])
    width = out_ref.shape[1] // 2
    for side in range(2):
        total = None
        for at, piece in enumerate(pieces):
            term = dot(x_ref[at], side_of(piece, side), 1, 0)
            total = term if total is None else total + term
        out_ref[:, side * width : (side + 1) * width] = total.astype(out_ref.dtype)


def project(x_blocks, pieces):
    lengths = [len(piece) for piece in pieces]
    flat = [part for piece in pieces for part in piece]
    tok_dev, width = x_blocks.shape[1], pieces[0][0].shape[1]
    return pl.pallas_call(
        functools.partial(project_kernel, lengths),
        out_shape=jax.ShapeDtypeStruct((tok_dev, width), jnp.bfloat16),
        in_specs=[vmem()] * (1 + len(flat)),
        out_specs=vmem(),
        compiler_params=params(),
        name="project",
    )(x_blocks, *flat)


def attend_kernel(sizes, info_ref, q_ref, g_ref, *refs):
    act_total, blocks_dev, seq_count, group, has_alias = sizes
    kv_refs = refs[: 2 * seq_count]
    refs = refs[2 * seq_count + (1 if has_alias else 0) :]
    dq_ref, own_ref = refs[0], refs[1]
    send_refs = refs[2 : 1 + seq_count]
    k_scr, v_scr, dk_scr, dv_scr = refs[1 + seq_count :]
    head = pl.program_id(0)
    width = own_ref.shape[1] // 2
    key_count = act_total * BLK
    scale = 1.0 / math.sqrt(HEAD_SIZE)
    columns = [pl.ds(pl.multiple_of(side * width + head * HEAD_SIZE, HEAD_SIZE), HEAD_SIZE) for side in range(2)]
    dk_scr[...] = jnp.zeros_like(dk_scr)
    dv_scr[...] = jnp.zeros_like(dv_scr)
    for slot in range(act_total):
        steps = info_ref[slot]
        row = pl.multiple_of(info_ref[act_total + slot] * BLK, BLK)
        rows = slice(slot * BLK, (slot + 1) * BLK)

        @pl.when(steps < 0)
        def _():
            k_scr[rows, :] = jnp.zeros((BLK, HEAD_SIZE), k_scr.dtype)
            v_scr[rows, :] = jnp.zeros((BLK, HEAD_SIZE), v_scr.dtype)

        for step in range(seq_count):

            @pl.when(steps == step)
            def _():
                k_scr[rows, :] = kv_refs[2 * step][pl.ds(row, BLK), :]
                v_scr[rows, :] = kv_refs[2 * step + 1][pl.ds(row, BLK), :]

    for block in range(blocks_dev):
        rank = info_ref[2 * act_total + block]
        rows = slice(block * BLK, (block + 1) * BLK)

        @pl.when(rank < 0)
        def _():
            dq_ref[rows, :] = jnp.zeros((BLK, group * HEAD_SIZE), dq_ref.dtype)

        @pl.when(rank >= 0)
        def _():
            keys, values = k_scr[...], v_scr[...]
            query = jnp.concatenate(
                [q_ref[rows, at * HEAD_SIZE : (at + 1) * HEAD_SIZE] for at in range(group)], axis=0
            )
            gradient = jnp.concatenate(
                [g_ref[rows, at * HEAD_SIZE : (at + 1) * HEAD_SIZE] for at in range(group)], axis=0
            )
            scores = dot(keys, query, 1, 1)
            shape = scores.shape
            key_pos = lax.broadcasted_iota(jnp.int32, shape, 0)
            query_pos = rank * BLK + (lax.broadcasted_iota(jnp.int32, shape, 1) & (BLK - 1))
            scores = jnp.where(key_pos <= query_pos, scores, MASKED)
            top = jnp.max(scores, axis=0, keepdims=True)
            exponent = jnp.exp((scores - top) * scale)
            probs = exponent * (1.0 / jnp.sum(exponent, axis=0, keepdims=True))
            probs_low = probs.astype(jnp.bfloat16)
            dprobs = dot(values, gradient, 1, 1)
            delta = jnp.sum(probs_low.astype(jnp.float32) * dprobs, axis=0, keepdims=True)
            dscores = (probs * (dprobs - delta) * scale).astype(jnp.bfloat16)
            dk_scr[...] += dot(dscores, query, 1, 0)
            dv_scr[...] += dot(probs_low, gradient, 1, 0)
            dquery = dot(keys, dscores, 0, 0).T.astype(dq_ref.dtype)
            for at in range(group):
                dq_ref[rows, at * HEAD_SIZE : (at + 1) * HEAD_SIZE] = dquery[at * BLK : (at + 1) * BLK]

    for target in (own_ref, *send_refs):
        for side in range(2):
            target[:, columns[side]] = jnp.zeros((target.shape[0], HEAD_SIZE), target.dtype)
    for slot in range(act_total):
        steps = info_ref[slot]
        row = pl.multiple_of(info_ref[act_total + slot] * BLK, BLK)
        rows = slice(slot * BLK, (slot + 1) * BLK)
        for step, target in enumerate((own_ref, *send_refs)):

            @pl.when(steps == step)
            def _():
                target[pl.ds(row, BLK), columns[0]] = dk_scr[rows, :].astype(target.dtype)
                target[pl.ds(row, BLK), columns[1]] = dv_scr[rows, :].astype(target.dtype)


def attend(info, queries, cotangent, kv_steps, chunk, heads, group, act_total, dq_so_far):
    seq_count = len(kv_steps)
    tok_dev, width = kv_steps[0].shape
    qwidth = queries.shape[2]
    group_width = group * HEAD_SIZE
    q_spec = pl.BlockSpec((None, tok_dev, group_width), lambda i: (0, 0, chunk * heads + i))
    kv_specs = [
        pl.BlockSpec((tok_dev, HEAD_SIZE), lambda i: (0, i)),
        pl.BlockSpec((tok_dev, HEAD_SIZE), lambda i: (0, heads + i)),
    ]
    whole_spec = pl.BlockSpec((tok_dev, width), lambda i: (0, 0))
    sizes = (act_total, tok_dev // BLK, seq_count, group, dq_so_far is not None)
    operands = [info, queries, cotangent, *[kv for kv in kv_steps for _ in range(2)]]
    in_specs = [smem(), q_spec, q_spec] + kv_specs * seq_count
    aliases = {}
    if dq_so_far is not None:
        aliases = {len(operands): 0}
        operands.append(dq_so_far)
        in_specs.append(pl.BlockSpec(memory_space=pl.ANY))
    outs = pl.pallas_call(
        functools.partial(attend_kernel, sizes),
        grid=(heads,),
        out_shape=[
            jax.ShapeDtypeStruct((1, tok_dev, qwidth), jnp.bfloat16),
            jax.ShapeDtypeStruct((tok_dev, width), jnp.float32),
            *[jax.ShapeDtypeStruct((tok_dev, width), jnp.bfloat16) for _ in range(seq_count - 1)],
        ],
        in_specs=in_specs,
        out_specs=[q_spec] + [whole_spec] * seq_count,
        scratch_shapes=[pltpu.VMEM((act_total * BLK, HEAD_SIZE), jnp.bfloat16)] * 2
        + [pltpu.VMEM((act_total * BLK, HEAD_SIZE), jnp.float32)] * 2,
        input_output_aliases=aliases,
        compiler_params=params(),
        name="attend",
    )(*operands)
    return outs[0], outs[1], outs[2:]


def token_kernel(lengths, chunk_count, *refs):
    out_ref = refs[-1]
    dkv_refs = refs[:chunk_count]
    per_chunk = sum(lengths)
    chunks = [
        unflatten(lengths, refs[chunk_count + at * per_chunk : chunk_count + (at + 1) * per_chunk])
        for at in range(chunk_count)
    ]
    width = dkv_refs[0].shape[1] // 2
    for at in range(len(lengths)):
        total = None
        for dkv_ref, pieces in zip(dkv_refs, chunks):
            for side in range(2):
                term = dot(dkv_ref[:, side * width : (side + 1) * width], side_of(pieces[at], side), 1, 1)
                total = term if total is None else total + term
        out_ref[at] = total.astype(out_ref.dtype)


def token_blocks(dkvs, weight_pieces):
    lengths = [len(piece) for piece in weight_pieces[0]]
    flat = [part for pieces in weight_pieces for piece in pieces for part in piece]
    rows = weight_pieces[0][0][0].shape[0]
    tok_dev = dkvs[0].shape[0]
    return pl.pallas_call(
        functools.partial(token_kernel, lengths, len(dkvs)),
        out_shape=jax.ShapeDtypeStruct((len(lengths), tok_dev, rows), jnp.bfloat16),
        in_specs=[vmem()] * (len(dkvs) + len(flat)),
        out_specs=vmem(),
        compiler_params=params(),
        name="token_grads",
    )(*dkvs, *flat)


def weight_kernel(lengths, dests, rank_ref, *refs):
    count = len(lengths)
    x_refs, refs = refs[:count], refs[count:]
    pieces = unflatten(lengths, refs[: sum(lengths)])
    own_ref, send_refs = refs[sum(lengths)], refs[sum(lengths) + 1 :]
    rank = rank_ref[0]
    column = own_ref.shape[1]
    totals = []
    for side in range(2):
        total = None
        for x_ref, piece in zip(x_refs, pieces):
            term = dot(x_ref[...], side_of(piece, side), 0, 0)
            total = term if total is None else total + term
        totals.append(total)
    own_ref[...] = jnp.zeros_like(own_ref)
    for dest, side, offset in dests:
        part = totals[side][:, offset : offset + column]

        @pl.when(rank == dest)
        def _():
            own_ref[...] = part

        for at, send_ref in enumerate(send_refs):

            @pl.when(rank ^ (at + 1) == dest)
            def _():
                send_ref[...] = part.astype(send_ref.dtype)


def weight_terms(rank, x_pieces, dkv_pieces, dests, column):
    lengths = [len(piece) for piece in dkv_pieces]
    flat = [part for piece in dkv_pieces for part in piece]
    seq_count = lax.axis_size("seq")
    rows = x_pieces[0].shape[1]
    outs = pl.pallas_call(
        functools.partial(weight_kernel, lengths, dests),
        out_shape=[jax.ShapeDtypeStruct((rows, column), jnp.float32)]
        + [jax.ShapeDtypeStruct((rows, column), jnp.bfloat16)] * (seq_count - 1),
        in_specs=[smem()] + [vmem()] * (len(x_pieces) + len(flat)),
        out_specs=[vmem()] * seq_count,
        compiler_params=params(),
        name="weight_grad",
    )(rank, *x_pieces, *flat)
    return outs[0], outs[1:]


def body(tokens, queries, cotangent, kv_weight, active):
    seq_count, dp_count = lax.axis_size("seq"), lax.axis_size("dp")
    seq_rank, dp_rank = lax.axis_index("seq"), lax.axis_index("dp")
    tok_dev, model = tokens.shape[1], tokens.shape[2]
    qwidth, kvwidth = queries.shape[2], kv_weight.shape[1]
    rows = kv_weight.shape[0]
    act_total = active.shape[1]
    kv_heads = kvwidth // (2 * HEAD_SIZE)
    group = qwidth // (HEAD_SIZE * kv_heads)
    heads = kv_heads // CHUNKS
    width = heads * HEAD_SIZE
    blocks_dev = tok_dev // BLK
    column = kvwidth // seq_count

    block_ids = active[0]
    local_ids = seq_rank * blocks_dev + jnp.arange(blocks_dev, dtype=jnp.int32)
    match = (block_ids[None, :] == local_ids[:, None]).astype(jnp.int32)
    slot_rank = jnp.sum(match * jnp.arange(1, act_total + 1, dtype=jnp.int32)[None, :], axis=1) - 1
    info = jnp.concatenate(
        [seq_rank - block_ids // blocks_dev, block_ids % blocks_dev, slot_rank]
    ).astype(jnp.int32)
    rank = seq_rank.astype(jnp.int32).reshape(1)

    others = dp_rank ^ jnp.arange(dp_count, dtype=jnp.int32)
    x_blocks = jnp.stack(
        [lax.dynamic_slice_in_dim(tokens[0], others[m] * rows, rows, axis=1) for m in range(dp_count)]
    )

    dq = None
    weight_pieces, owns = [], []
    dkvs, terms = [], []
    for chunk in range(CHUNKS):
        key_at, value_at = chunk * width, (kv_heads // CHUNKS * CHUNKS) * HEAD_SIZE + chunk * width
        shard = jnp.concatenate(
            [kv_weight[:, key_at : key_at + width], kv_weight[:, value_at : value_at + width]], axis=1
        )
        weight_pieces.append(gather_pieces(shard))
    x_pieces = [x_blocks[0]] + [exchange(x_blocks[m], "dp", m) for m in range(1, dp_count)]
    for chunk in range(CHUNKS):
        keyval = project(x_blocks, weight_pieces[chunk])
        kv_steps = [keyval] + [moved(keyval, "seq", step) for step in range(1, seq_count)]
        dq, own, sends = attend(
            info, queries, cotangent, kv_steps, chunk, heads, group, act_total, dq
        )
        total = own
        for step, send in enumerate(sends):
            total = total + moved(send, "seq", -(step + 1)).astype(jnp.float32)
        dkvs.append(total.astype(jnp.bfloat16))
    for chunk in range(CHUNKS):
        dkv_pieces = gather_pieces(dkvs[chunk])
        dests = []
        for side in range(2):
            start = side * (kvwidth // 2) + chunk * width
            for offset in range(0, width, column):
                dests.append(((start + offset) // column, side, offset))
        own, sends = weight_terms(rank, x_pieces, dkv_pieces, dests, column)
        terms.append(own)
        for at, send in enumerate(sends):
            pairs = [(dest ^ (at + 1), dest) for dest, _, _ in dests]
            terms.append(lax.ppermute(send, "seq", pairs).astype(jnp.float32))
    weight_grad = functools.reduce(lambda a, b: a + b, terms)
    blocks = token_blocks(dkvs, weight_pieces)
    token_grad = jnp.concatenate(
        [lax.dynamic_index_in_dim(blocks, others[m], axis=0, keepdims=False) for m in range(dp_count)], axis=1
    )
    return (dq, token_grad[None], weight_grad)


def solution(mesh):
    in_specs = (
        P("dp", "seq", None),
        P("dp", "seq", None),
        P("dp", "seq", None),
        P("dp", None),
        P("dp", None),
    )
    out_specs = (P("dp", "seq", None), P("dp", "seq", None), P("dp", "seq"))
    return jax.shard_map(body, mesh=mesh, in_specs=in_specs, out_specs=out_specs, check_vma=False)
```

```python
import functools
import math

import jax
import jax.numpy as jnp
from jax import lax
from jax.experimental import pallas as pl
from jax.experimental.pallas import tpu as pltpu
from jax.sharding import PartitionSpec as P

HEAD_SIZE = 128
BLK = 128
CHUNKS = 2
PARTS = 1
VMEM_BYTES = 56 * 1024 * 1024
MASKED = -1e30


def params():
    return pltpu.CompilerParams(vmem_limit_bytes=VMEM_BYTES)


def lasting(microseconds):
    return pl.CostEstimate(flops=4000000000 * microseconds, bytes_accessed=12000000 * microseconds, transcendentals=0)


def vmem():
    return pl.BlockSpec(memory_space=pltpu.VMEM)


def smem():
    return pl.BlockSpec(memory_space=pltpu.SMEM)


def dot(left, right, left_dim, right_dim):
    return lax.dot_general(
        left, right, (((left_dim,), (right_dim,)), ((), ())), preferred_element_type=jnp.float32
    )


def exchange(value, axis, mask):
    count = lax.axis_size(axis)
    return lax.ppermute(value, axis, [(i, i ^ mask) for i in range(count)])


def moved(value, axis, step, first=0):
    count = lax.axis_size(axis)
    pairs = [(i, i + step) for i in range(first, count) if 0 <= i + step < count]
    return lax.ppermute(value, axis, pairs)


def spread(value):
    count = lax.axis_size("seq")
    steps = [value] + [None] * (count - 1)
    for step in range(2, count, 2):
        steps[step] = moved(steps[step - 2], "seq", 2, step - 2)
    for step in range(1, count, 2):
        steps[step] = moved(steps[step - 1], "seq", 1, step - 1)
    return steps


def added(left, right):
    return (left.astype(jnp.float32) + right.astype(jnp.float32)).astype(left.dtype)


def collect(sends, gates, later):
    count = lax.axis_size("seq")
    sends = [None, *sends]
    sends = [None] + [after(send, *gates) for send in sends[1:]]
    arrived = []
    for step in range(3, count, 2):
        arrived.append(moved(sends[step], "seq", -1, step))
        sends[step - 1] = added(sends[step - 1], arrived[-1])
    if len(sends) > 2:
        sends[2] = after(sends[2], *later)
    for step in range((count - 1) // 2 * 2, 2, -2):
        sends[step - 2] = added(sends[step - 2], moved(sends[step], "seq", -2, step))
    return arrived, [moved(sends[step], "seq", -step, step) for step in (1, 2) if step < count]


def gather_direct(own):
    count = lax.axis_size("dp")
    pieces = [own] + [None] * (count - 1)
    for mask in range(2, count, 2):
        pieces[mask] = exchange(own, "dp", mask)
    for mask in range(0, count, 2):
        pieces[mask + 1] = exchange(pieces[mask], "dp", 1)
    return pieces


def after(value, *others):
    return lax.optimization_barrier((value, others))[0]


def side_of(table, refs, at, side):
    array, start, width = table[at][side]
    return refs[array][:, start : start + width]


def whole_table(count, width):
    return tuple(((at, 0, width), (at, width, width)) for at in range(count))


def gather_weights(shards, behind, use_first):
    count = lax.axis_size("dp")
    width = shards[0].shape[1] // 2
    if count != 8 or len(shards) != 2:
        result = []
        for shard in shards:
            pieces = gather_direct(shard)
            result.append((pieces, whole_table(count, width)))
        return result, [use_first(result[0])], pieces[-1:]
    left, right = slice(0, width), slice(width, 2 * width)
    first, second = shards
    from_x, from_y = exchange(first, "dp", 2), exchange(first, "dp", 4)
    here, there = after(from_x, *behind), after(from_y, *behind)
    step_y = exchange(jnp.concatenate([here[:, left], second[:, left]], axis=1), "dp", 4)
    step_x = exchange(jnp.concatenate([there[:, right], second[:, right]], axis=1), "dp", 2)
    last_x = exchange(jnp.concatenate([step_y[:, right], second[:, left]], axis=1), "dp", 2)
    last_y = exchange(jnp.concatenate([step_x[:, right], second[:, right]], axis=1), "dp", 4)
    near = [first, from_x, from_y, step_y, step_x]
    near_core = [exchange(part, "dp", 1) for part in near]
    one = [((0, 0), (0, 1)), ((1, 0), (1, 1)), ((2, 0), (2, 1)), ((3, 0), (4, 0))]
    two = [((0, 0), (0, 1)), ((1, 1), (4, 1)), ((3, 1), (2, 1)), ((1, 0), (2, 0))]
    tables = []
    for entries in (one, two):
        table = []
        for entry in entries:
            for core in range(2):
                table.append(tuple((array + core * 5, part * width, width) for array, part in entry))
        tables.append(tuple(table))
    pieces = [(near + near_core, tables[0])]
    used = use_first(pieces[0])
    last_x, last_y = after((last_x, last_y), used[min(2, len(used) - 1)])
    far = [second, last_x, last_y]
    far_core = [exchange(part, "dp", 1) for part in far]
    pieces.append((far + [step_y, step_x] + far_core + near_core[3:], tables[1]))
    return pieces, [used], (last_x, last_y)


def split_kernel(x_ref, *out_refs):
    for at, out_ref in enumerate(out_refs):
        height = out_ref.shape[0]
        out_ref[...] = x_ref[at * height : (at + 1) * height]


def split_columns(tokens, count):
    tok_dev, model = tokens.shape[1:]
    rows, height = model // count, tok_dev // PARTS
    if rows % 128:
        return [
            jnp.stack([tokens[0, part * height : (part + 1) * height, at * rows : (at + 1) * rows] for at in range(count)])
            for part in range(PARTS)
        ]
    return pl.pallas_call(
        split_kernel,
        grid=(count,),
        out_shape=[jax.ShapeDtypeStruct((count, height, rows), tokens.dtype)] * PARTS,
        in_specs=[pl.BlockSpec((None, tok_dev, rows), lambda at: (0, 0, at))],
        out_specs=[pl.BlockSpec((None, height, rows), lambda at: (at, 0, 0))] * PARTS,
        compiler_params=params(),
        cost_estimate=lasting(3),
        name="split_columns",
    )(tokens)


def rows_of(x_refs, owner):
    return jnp.concatenate([x_ref[owner] for x_ref in x_refs], axis=0)


def project_kernel(table, rank_ref, *refs):
    x_refs, refs, out_ref = refs[:PARTS], refs[PARTS:-1], refs[-1]
    width = out_ref.shape[1] // 2
    totals = [None, None]
    for at in range(len(table)):
        rows = rows_of(x_refs, rank_ref[1] ^ at)
        for side in range(2):
            term = dot(rows, side_of(table, refs, at, side), 1, 0)
            totals[side] = term if totals[side] is None else totals[side] + term
    for side in range(2):
        out_ref[:, side * width : (side + 1) * width] = totals[side].astype(out_ref.dtype)


def project(rank, x_by_owner, pieces):
    arrays, table = pieces
    tok_dev, width = x_by_owner[0].shape[1] * PARTS, table[0][0][2] * 2
    return pl.pallas_call(
        functools.partial(project_kernel, table),
        out_shape=jax.ShapeDtypeStruct((tok_dev, width), jnp.bfloat16),
        in_specs=[smem()] + [vmem()] * (PARTS + len(arrays)),
        out_specs=vmem(),
        compiler_params=params(),
        cost_estimate=lasting(4),
        name="project",
    )(rank, *x_by_owner, *arrays)


def attend_kernel(sizes, info_ref, q_ref, g_ref, *refs):
    act_total, blocks_dev, seq_count, group, has_alias = sizes
    kv_refs = refs[: 2 * seq_count]
    refs = refs[2 * seq_count + (1 if has_alias else 0) :]
    dq_ref, own_ref = refs[0], refs[1]
    send_refs = refs[2 : 1 + seq_count]
    k_scr, v_scr, dk_scr, dv_scr = refs[1 + seq_count :]
    head = pl.program_id(0)
    width = own_ref.shape[1] // 2
    key_count = act_total * BLK
    scale = 1.0 / math.sqrt(HEAD_SIZE)
    columns = [pl.ds(pl.multiple_of(side * width + head * HEAD_SIZE, HEAD_SIZE), HEAD_SIZE) for side in range(2)]
    dk_scr[...] = jnp.zeros_like(dk_scr)
    dv_scr[...] = jnp.zeros_like(dv_scr)
    for slot in range(act_total):
        steps = info_ref[slot]
        row = pl.multiple_of(info_ref[act_total + slot] * BLK, BLK)
        rows = slice(slot * BLK, (slot + 1) * BLK)

        @pl.when(steps < 0)
        def _():
            k_scr[rows, :] = jnp.zeros((BLK, HEAD_SIZE), k_scr.dtype)
            v_scr[rows, :] = jnp.zeros((BLK, HEAD_SIZE), v_scr.dtype)

        for step in range(seq_count):

            @pl.when(steps == step)
            def _():
                k_scr[rows, :] = kv_refs[2 * step][pl.ds(row, BLK), :]
                v_scr[rows, :] = kv_refs[2 * step + 1][pl.ds(row, BLK), :]

    for block in range(blocks_dev):
        rank = info_ref[2 * act_total + block]
        rows = slice(block * BLK, (block + 1) * BLK)

        @pl.when(rank < 0)
        def _():
            dq_ref[rows, :] = jnp.zeros((BLK, group * HEAD_SIZE), dq_ref.dtype)

        @pl.when(rank >= 0)
        def _():
            keys, values = k_scr[...], v_scr[...]
            query = jnp.concatenate(
                [q_ref[rows, at * HEAD_SIZE : (at + 1) * HEAD_SIZE] for at in range(group)], axis=0
            )
            gradient = jnp.concatenate(
                [g_ref[rows, at * HEAD_SIZE : (at + 1) * HEAD_SIZE] for at in range(group)], axis=0
            )
            scores = dot(keys, query, 1, 1)
            shape = scores.shape
            key_pos = lax.broadcasted_iota(jnp.int32, shape, 0)
            query_pos = rank * BLK + (lax.broadcasted_iota(jnp.int32, shape, 1) & (BLK - 1))
            scores = jnp.where(key_pos <= query_pos, scores, MASKED)
            top = jnp.max(scores, axis=0, keepdims=True)
            exponent = jnp.exp((scores - top) * scale)
            probs = exponent * (1.0 / jnp.sum(exponent, axis=0, keepdims=True))
            probs_low = probs.astype(jnp.bfloat16)
            dprobs = dot(values, gradient, 1, 1)
            delta = jnp.sum(probs_low.astype(jnp.float32) * dprobs, axis=0, keepdims=True)
            dscores = (probs * (dprobs - delta) * scale).astype(jnp.bfloat16)
            dk_scr[...] += dot(dscores, query, 1, 0)
            dv_scr[...] += dot(probs_low, gradient, 1, 0)
            dquery = dot(keys, dscores, 0, 0).T.astype(dq_ref.dtype)
            for at in range(group):
                dq_ref[rows, at * HEAD_SIZE : (at + 1) * HEAD_SIZE] = dquery[at * BLK : (at + 1) * BLK]

    for target in (own_ref, *send_refs):
        for side in range(2):
            target[:, columns[side]] = jnp.zeros((target.shape[0], HEAD_SIZE), target.dtype)
    for slot in range(act_total):
        steps = info_ref[slot]
        row = pl.multiple_of(info_ref[act_total + slot] * BLK, BLK)
        rows = slice(slot * BLK, (slot + 1) * BLK)
        for step, target in enumerate((own_ref, *send_refs)):

            @pl.when(steps == step)
            def _():
                target[pl.ds(row, BLK), columns[0]] = dk_scr[rows, :].astype(target.dtype)
                target[pl.ds(row, BLK), columns[1]] = dv_scr[rows, :].astype(target.dtype)


def attend(info, queries, cotangent, kv_steps, chunk, heads, group, act_total, dq_so_far):
    seq_count = len(kv_steps)
    tok_dev, width = kv_steps[0].shape
    qwidth = queries.shape[2]
    group_width = group * HEAD_SIZE
    q_spec = pl.BlockSpec((None, tok_dev, group_width), lambda i: (0, 0, chunk * heads + i))
    kv_specs = [
        pl.BlockSpec((tok_dev, HEAD_SIZE), lambda i: (0, i)),
        pl.BlockSpec((tok_dev, HEAD_SIZE), lambda i: (0, heads + i)),
    ]
    whole_spec = pl.BlockSpec((tok_dev, width), lambda i: (0, 0))
    sizes = (act_total, tok_dev // BLK, seq_count, group, dq_so_far is not None)
    operands = [info, queries, cotangent, *[kv for kv in kv_steps for _ in range(2)]]
    in_specs = [smem(), q_spec, q_spec] + kv_specs * seq_count
    aliases = {}
    if dq_so_far is not None:
        aliases = {len(operands): 0}
        operands.append(dq_so_far)
        in_specs.append(pl.BlockSpec(memory_space=pl.ANY))
    outs = pl.pallas_call(
        functools.partial(attend_kernel, sizes),
        grid=(heads,),
        out_shape=[
            jax.ShapeDtypeStruct((1, tok_dev, qwidth), jnp.bfloat16),
            jax.ShapeDtypeStruct((tok_dev, width), jnp.float32),
            *[jax.ShapeDtypeStruct((tok_dev, width), jnp.bfloat16) for _ in range(seq_count - 1)],
        ],
        in_specs=in_specs,
        out_specs=[q_spec] + [whole_spec] * seq_count,
        scratch_shapes=[pltpu.VMEM((act_total * BLK, HEAD_SIZE), jnp.bfloat16)] * 2
        + [pltpu.VMEM((act_total * BLK, HEAD_SIZE), jnp.float32)] * 2,
        input_output_aliases=aliases,
        compiler_params=params(),
        cost_estimate=lasting(9),
        name="attend",
    )(*operands)
    return outs[0], outs[1], outs[2:]


def token_kernel(tables, indices, rank_ref, *refs):
    out_ref = refs[-1]
    dkv_refs, refs = refs[: len(tables)], refs[len(tables) : -1]
    width = dkv_refs[0].shape[1] // 2
    count = len(tables[0])
    rows = out_ref.shape[-1] if len(out_ref.shape) == 3 else out_ref.shape[1] // count
    for at in range(count):
        owner = rank_ref[1] ^ at
        total = None
        for dkv_ref, table, index in zip(dkv_refs, tables, indices):
            arrays = [refs[number] for number in index]
            for side in range(2):
                term = dot(
                    dkv_ref[:, side * width : (side + 1) * width], side_of(table, arrays, at, side), 1, 1
                )
                total = term if total is None else total + term
        if len(out_ref.shape) == 3:
            out_ref[owner] = total.astype(out_ref.dtype)
        else:
            out_ref[:, pl.ds(pl.multiple_of(owner * rows, 128), rows)] = total.astype(out_ref.dtype)


def token_grads(rank, dkvs, weight_pieces, rows):
    flat, indices = [], []
    for arrays, _ in weight_pieces:
        index = []
        for array in arrays:
            known = [at for at, other in enumerate(flat) if other is array]
            if not known:
                known = [len(flat)]
                flat.append(array)
            index.append(known[0])
        indices.append(tuple(index))
    tables = tuple(table for _, table in weight_pieces)
    count = lax.axis_size("dp")
    tok_dev = dkvs[0].shape[0]
    flat_out = rows % 128 == 0
    shape = (tok_dev, count * rows) if flat_out else (count, tok_dev, rows)
    out = pl.pallas_call(
        functools.partial(token_kernel, tables, tuple(indices)),
        out_shape=jax.ShapeDtypeStruct(shape, jnp.bfloat16),
        in_specs=[smem()] + [vmem()] * (len(dkvs) + len(flat)),
        out_specs=vmem(),
        compiler_params=params(),
        cost_estimate=lasting(8),
        name="token_grads",
    )(rank, *dkvs, *flat)
    return out if flat_out else jnp.concatenate(list(out), axis=1)


def weight_kernel(dests, has_before, rank_ref, *refs):
    x_refs, refs = refs[:PARTS], refs[PARTS:]
    count = x_refs[0].shape[0]
    pieces, refs = refs[:count], refs[count:]
    out_refs = refs[len(refs) // 2 :] if has_before else refs
    column, width = out_refs[0].shape[1], pieces[0].shape[1] // 2
    totals = [None, None]
    for at in range(count):
        rows = rows_of(x_refs, rank_ref[1] ^ at)
        for side in range(2):
            term = dot(rows, pieces[at][:, side * width : (side + 1) * width], 0, 0)
            totals[side] = term if totals[side] is None else totals[side] + term
    for at, out_ref in enumerate(out_refs):
        if has_before:
            out_ref[...] = refs[at][...]
        for dest, side, offset in dests:

            @pl.when(rank_ref[0] ^ at == dest)
            def _():
                out_ref[...] = totals[side][:, offset : offset + column].astype(out_ref.dtype)


def weight_terms(rank, x_all, pieces, dests, column, before):
    seq_count = lax.axis_size("seq")
    rows = x_all[0].shape[2]
    operands = [*x_all, *pieces, *before]
    return pl.pallas_call(
        functools.partial(weight_kernel, dests, bool(before)),
        out_shape=[jax.ShapeDtypeStruct((rows, column), jnp.float32)]
        + [jax.ShapeDtypeStruct((rows, column), jnp.bfloat16)] * (seq_count - 1),
        in_specs=[smem()] + [vmem()] * len(operands),
        out_specs=[vmem()] * seq_count,
        compiler_params=params(),
        cost_estimate=lasting(4),
        name="weight_grad",
    )(rank, *operands)


def body(tokens, queries, cotangent, kv_weight, active):
    seq_count, dp_count = lax.axis_size("seq"), lax.axis_size("dp")
    seq_rank, dp_rank = lax.axis_index("seq"), lax.axis_index("dp")
    tok_dev, model = tokens.shape[1], tokens.shape[2]
    qwidth, kvwidth = queries.shape[2], kv_weight.shape[1]
    rows = kv_weight.shape[0]
    act_total = active.shape[1]
    kv_heads = kvwidth // (2 * HEAD_SIZE)
    group = qwidth // (HEAD_SIZE * kv_heads)
    heads = kv_heads // CHUNKS
    width = heads * HEAD_SIZE
    blocks_dev = tok_dev // BLK
    column = kvwidth // seq_count

    block_ids = active[0]
    local_ids = seq_rank * blocks_dev + jnp.arange(blocks_dev, dtype=jnp.int32)
    match = (block_ids[None, :] == local_ids[:, None]).astype(jnp.int32)
    slot_rank = jnp.sum(match * jnp.arange(1, act_total + 1, dtype=jnp.int32)[None, :], axis=1) - 1
    info = jnp.concatenate(
        [seq_rank - block_ids // blocks_dev, block_ids % blocks_dev, slot_rank]
    ).astype(jnp.int32)
    rank = jnp.stack([seq_rank, dp_rank]).astype(jnp.int32)

    x_by_owner = split_columns(tokens, dp_count)

    dq = None
    dkvs, terms = [], []
    shards = []
    for chunk in range(CHUNKS):
        key_at, value_at = chunk * width, kvwidth // 2 + chunk * width
        shards.append(
            jnp.concatenate(
                [kv_weight[:, key_at : key_at + width], kv_weight[:, value_at : value_at + width]], axis=1
            )
        )
    weight_pieces, keyvals, weight_gates = gather_weights(
        shards, x_by_owner, lambda pieces: spread(project(rank, x_by_owner, pieces))
    )
    arrivals, keyvals = [steps[1:] for steps in keyvals], [steps[0] for steps in keyvals]
    for chunk in range(1, CHUNKS):
        waits = arrivals[-1][1:2]
        keyvals.append(project(after(rank, *waits), x_by_owner, weight_pieces[chunk]))
        arrivals.append(spread(keyvals[-1])[1:])
    x_all, gates = [], weight_gates
    for part in x_by_owner:
        part = lax.all_to_all(after(part, *gates), "dp", split_axis=0, concat_axis=0, tiled=True)
        x_all.append(part)
        gates = (part,)

    backs, owns = [], []
    gates, waits, later = (keyvals[-1],), tuple(arrivals[-1][1:2]), tuple(x_all)
    for chunk in range(CHUNKS):
        kv_steps = [keyvals[chunk]] + arrivals[chunk]
        dq, own, sends = attend(
            after(info, *gates), queries, cotangent, kv_steps, chunk, heads, group, act_total, dq
        )
        arrived, back = collect(sends, waits, later)
        backs.append(back)
        owns.append(own)
        gates, waits, later = tuple(arrived), tuple(back), ()
    gates, sums = tuple(arrived), ()
    for chunk in range(CHUNKS):
        total = after(owns[chunk], *gates)
        for part in backs[chunk]:
            total = total + part.astype(jnp.float32)
        dkvs.append(total.astype(jnp.bfloat16))
        dkv_pieces = gather_direct(dkvs[chunk])
        dests = []
        for side in range(2):
            start = side * (kvwidth // 2) + chunk * width
            for offset in range(0, width, column):
                dests.append(((start + offset) // column, side, offset))
        sums = weight_terms(rank, x_all, dkv_pieces, dests, column, sums)
        gates = ()
    gates = (sums[0],)
    terms = [sums[0]]
    for at, send in enumerate(sums[1:]):
        terms.append(exchange(send, "seq", at + 1).astype(jnp.float32))
    weight_grad = functools.reduce(lambda a, b: a + b, terms)
    token_grad = token_grads(after(rank, *gates), dkvs, weight_pieces, rows)
    return (dq, token_grad[None], weight_grad)


def solution(mesh):
    in_specs = (
        P("dp", "seq", None),
        P("dp", "seq", None),
        P("dp", "seq", None),
        P("dp", None),
        P("dp", None),
    )
    out_specs = (P("dp", "seq", None), P("dp", "seq", None), P("dp", "seq"))
    return jax.shard_map(body, mesh=mesh, in_specs=in_specs, out_specs=out_specs, check_vma=False)
```

```python
import functools
import math

import jax
import jax.numpy as jnp
from jax import lax
from jax.experimental import pallas as pl
from jax.experimental.pallas import tpu as pltpu
from jax.sharding import PartitionSpec as P

HEAD_SIZE = 128
BLK = 128
CHUNKS = 2
PARTS = 1
VMEM_BYTES = 24 * 1024 * 1024
MASKED = -1e30


def params():
    return pltpu.CompilerParams(vmem_limit_bytes=VMEM_BYTES)


def lasting(microseconds):
    return pl.CostEstimate(flops=4000000000 * microseconds, bytes_accessed=12000000 * microseconds, transcendentals=0)


def vmem():
    return pl.BlockSpec(memory_space=pltpu.VMEM)


def smem():
    return pl.BlockSpec(memory_space=pltpu.SMEM)


def dot(left, right, left_dim, right_dim):
    return lax.dot_general(
        left, right, (((left_dim,), (right_dim,)), ((), ())), preferred_element_type=jnp.float32
    )


def exchange(value, axis, mask):
    count = lax.axis_size(axis)
    return lax.ppermute(value, axis, [(i, i ^ mask) for i in range(count)])


def moved(value, axis, step, first=0):
    count = lax.axis_size(axis)
    pairs = [(i, i + step) for i in range(first, count) if 0 <= i + step < count]
    return lax.ppermute(value, axis, pairs)


def spread(value):
    count = lax.axis_size("seq")
    steps = [value] + [None] * (count - 1)
    for step in range(2, count, 2):
        steps[step] = moved(steps[step - 2], "seq", 2, step - 2)
    if count > 1:
        steps[1] = moved(value, "seq", 1)
    return steps


def relay(value):
    steps = [value]
    for step in range(1, lax.axis_size("seq") - 1):
        steps.append(moved(steps[-1], "seq", 1, step - 1))
    return steps


def finish_relay(steps, *gates):
    return [*steps, moved(after(steps[-1], *gates), "seq", 1, len(steps) - 1)]


def finish(steps, *gates):
    for step in range(3, len(steps), 2):
        steps[step] = moved(after(steps[step - 1], *gates), "seq", 1, step - 1)
    return steps


def added(left, right):
    return (left.astype(jnp.float32) + right.astype(jnp.float32)).astype(left.dtype)


def collect(sends, gates, later):
    count = lax.axis_size("seq")
    sends = [None, *sends]
    sends = [None] + [after(send, *gates) for send in sends[1:]]
    arrived = []
    for step in range(3, count, 2):
        arrived.append(moved(sends[step], "seq", -1, step))
        sends[step - 1] = added(sends[step - 1], arrived[-1])
    if len(sends) > 2:
        sends[2] = after(sends[2], *later)
    for step in range((count - 1) // 2 * 2, 2, -2):
        sends[step - 2] = added(sends[step - 2], moved(sends[step], "seq", -2, step))
    return arrived, [moved(sends[step], "seq", -step, step) for step in (1, 2) if step < count]


def gather_direct(own, *gates):
    count = lax.axis_size("dp")
    pieces = [own] + [None] * (count - 1)
    for mask in range(2, count, 2):
        pieces[mask] = exchange(own, "dp", mask)
    for mask in range(0, count, 2):
        pieces[mask + 1] = exchange(after(pieces[mask], *gates), "dp", 1)
    return pieces


def gather_doubling(own, second, last):
    bit, stack = 2, own
    while bit < lax.axis_size("dp"):
        stack = jnp.concatenate([stack, exchange(stack, "dp", bit)], axis=0)
        if bit == 2:
            stack = after(stack, *second)
        bit *= 2
    return [stack, exchange(after(stack, *last), "dp", 1)]


def after(value, *others):
    return lax.optimization_barrier((value, others))[0]


def side_of(table, refs, at, side):
    array, start, width = table[at][side]
    return refs[array][:, start : start + width]


def whole_table(count, width):
    return tuple(((at, 0, width), (at, width, width)) for at in range(count))


def pack_kernel(near_ref, far_ref, own_ref, left_ref, right_ref, *, near_start, far_start):
    width = own_ref.shape[1] // 2
    left_ref[:, :width] = near_ref[:, near_start : near_start + width]
    left_ref[:, width:] = own_ref[:, :width]
    right_ref[:, :width] = far_ref[:, far_start : far_start + width]
    right_ref[:, width:] = own_ref[:, width:]


def pack(near, far, own, near_start, far_start):
    shape = jax.ShapeDtypeStruct(own.shape, own.dtype)
    return pl.pallas_call(
        functools.partial(pack_kernel, near_start=near_start, far_start=far_start),
        out_shape=[shape, shape],
        in_specs=[vmem()] * 3,
        out_specs=[vmem()] * 2,
        compiler_params=params(),
        cost_estimate=lasting(1),
        name="pack",
    )(near, far, own)


def gather_weights(shards, behind, use_first):
    count = lax.axis_size("dp")
    width = shards[0].shape[1] // 2
    if count != 8 or len(shards) != 2:
        result = []
        for shard in shards:
            pieces = gather_direct(shard)
            result.append((pieces, whole_table(count, width)))
        return result, [use_first(result[0])], pieces[-1:]
    first, second = shards
    from_x, from_y = exchange(first, "dp", 2), exchange(first, "dp", 4)
    here, there = after(from_x, *behind), after(from_y, *behind)
    to_y, to_x = pack(here, there, second, 0, width)
    step_y, step_x = exchange(to_y, "dp", 4), exchange(to_x, "dp", 2)
    to_x, to_y = pack(step_y, step_x, second, width, width)
    last_x, last_y = exchange(to_x, "dp", 2), exchange(to_y, "dp", 4)
    near = [first, from_x, from_y, step_y, step_x]
    near_core = [exchange(part, "dp", 1) for part in near]
    one = [((0, 0), (0, 1)), ((1, 0), (1, 1)), ((2, 0), (2, 1)), ((3, 0), (4, 0))]
    two = [((0, 0), (0, 1)), ((1, 1), (4, 1)), ((3, 1), (2, 1)), ((1, 0), (2, 0))]
    tables = []
    for entries in (one, two):
        table = []
        for entry in entries:
            for core in range(2):
                table.append(tuple((array + core * 5, part * width, width) for array, part in entry))
        tables.append(tuple(table))
    pieces = [(near + near_core, tables[0])]
    used = use_first(pieces[0])
    last_x, last_y = after((last_x, last_y), used[min(1, len(used) - 1)])
    far = [second, last_x, last_y]
    far_core = [exchange(part, "dp", 1) for part in far]
    pieces.append((far + [step_y, step_x] + far_core + near_core[3:], tables[1]))
    return pieces, [used], used[1:2]


def split_kernel(x_ref, *out_refs):
    for at, out_ref in enumerate(out_refs):
        height = out_ref.shape[0]
        out_ref[...] = x_ref[at * height : (at + 1) * height]


def split_columns(tokens, count):
    tok_dev, model = tokens.shape[1:]
    rows, height = model // count, tok_dev // PARTS
    if rows % 128:
        return [
            jnp.stack([tokens[0, part * height : (part + 1) * height, at * rows : (at + 1) * rows] for at in range(count)])
            for part in range(PARTS)
        ]
    return pl.pallas_call(
        split_kernel,
        grid=(count,),
        out_shape=[jax.ShapeDtypeStruct((count, height, rows), tokens.dtype)] * PARTS,
        in_specs=[pl.BlockSpec((None, tok_dev, rows), lambda at: (0, 0, at))],
        out_specs=[pl.BlockSpec((None, height, rows), lambda at: (at, 0, 0))] * PARTS,
        compiler_params=params(),
        cost_estimate=lasting(3),
        name="split_columns",
    )(tokens)


def rows_of(x_refs, owner):
    return jnp.concatenate([x_ref[owner] for x_ref in x_refs], axis=0)


def project_kernel(table, rank_ref, *refs):
    x_refs, refs, out_ref = refs[:PARTS], refs[PARTS:-1], refs[-1]
    width = out_ref.shape[1] // 2
    totals = [None, None]
    for at in range(len(table)):
        rows = rows_of(x_refs, rank_ref[1] ^ at)
        for side in range(2):
            term = dot(rows, side_of(table, refs, at, side), 1, 0)
            totals[side] = term if totals[side] is None else totals[side] + term
    for side in range(2):
        out_ref[:, side * width : (side + 1) * width] = totals[side].astype(out_ref.dtype)


def project(rank, x_by_owner, pieces):
    arrays, table = pieces
    tok_dev, width = x_by_owner[0].shape[1] * PARTS, table[0][0][2] * 2
    return pl.pallas_call(
        functools.partial(project_kernel, table),
        out_shape=jax.ShapeDtypeStruct((tok_dev, width), jnp.bfloat16),
        in_specs=[smem()] + [vmem()] * (PARTS + len(arrays)),
        out_specs=vmem(),
        compiler_params=params(),
        cost_estimate=lasting(4),
        name="project",
    )(rank, *x_by_owner, *arrays)


def attend_kernel(sizes, info_ref, q_ref, g_ref, *refs):
    act_total, blocks_dev, seq_count, group, has_alias = sizes
    kv_refs = refs[: 2 * seq_count]
    refs = refs[2 * seq_count + (1 if has_alias else 0) :]
    dq_ref, own_ref = refs[0], refs[1]
    send_refs = refs[2 : 1 + seq_count]
    k_scr, v_scr, dk_scr, dv_scr = refs[1 + seq_count :]
    head = pl.program_id(0)
    width = own_ref.shape[1] // 2
    key_count = act_total * BLK
    scale = 1.0 / math.sqrt(HEAD_SIZE)
    columns = [pl.ds(pl.multiple_of(side * width + head * HEAD_SIZE, HEAD_SIZE), HEAD_SIZE) for side in range(2)]
    dk_scr[...] = jnp.zeros_like(dk_scr)
    dv_scr[...] = jnp.zeros_like(dv_scr)
    for slot in range(act_total):
        steps = info_ref[slot]
        row = pl.multiple_of(info_ref[act_total + slot] * BLK, BLK)
        rows = slice(slot * BLK, (slot + 1) * BLK)

        @pl.when(steps < 0)
        def _():
            k_scr[rows, :] = jnp.zeros((BLK, HEAD_SIZE), k_scr.dtype)
            v_scr[rows, :] = jnp.zeros((BLK, HEAD_SIZE), v_scr.dtype)

        for step in range(seq_count):

            @pl.when(steps == step)
            def _():
                k_scr[rows, :] = kv_refs[2 * step][pl.ds(row, BLK), :]
                v_scr[rows, :] = kv_refs[2 * step + 1][pl.ds(row, BLK), :]

    for block in range(blocks_dev):
        rank = info_ref[2 * act_total + block]
        rows = slice(block * BLK, (block + 1) * BLK)

        @pl.when(rank < 0)
        def _():
            dq_ref[rows, :] = jnp.zeros((BLK, group * HEAD_SIZE), dq_ref.dtype)

        @pl.when(rank >= 0)
        def _():
            keys, values = k_scr[...], v_scr[...]
            query = jnp.concatenate(
                [q_ref[rows, at * HEAD_SIZE : (at + 1) * HEAD_SIZE] for at in range(group)], axis=0
            )
            gradient = jnp.concatenate(
                [g_ref[rows, at * HEAD_SIZE : (at + 1) * HEAD_SIZE] for at in range(group)], axis=0
            )
            scores = dot(keys, query, 1, 1)
            shape = scores.shape
            key_pos = lax.broadcasted_iota(jnp.int32, shape, 0)
            query_pos = rank * BLK + (lax.broadcasted_iota(jnp.int32, shape, 1) & (BLK - 1))
            scores = jnp.where(key_pos <= query_pos, scores, MASKED)
            top = jnp.max(scores, axis=0, keepdims=True)
            exponent = jnp.exp((scores - top) * scale)
            probs = exponent * (1.0 / jnp.sum(exponent, axis=0, keepdims=True))
            probs_low = probs.astype(jnp.bfloat16)
            dprobs = dot(values, gradient, 1, 1)
            delta = jnp.sum(probs_low.astype(jnp.float32) * dprobs, axis=0, keepdims=True)
            dscores = (probs * (dprobs - delta) * scale).astype(jnp.bfloat16)
            dk_scr[...] += dot(dscores, query, 1, 0)
            dv_scr[...] += dot(probs_low, gradient, 1, 0)
            dquery = dot(keys, dscores, 0, 0).T.astype(dq_ref.dtype)
            for at in range(group):
                dq_ref[rows, at * HEAD_SIZE : (at + 1) * HEAD_SIZE] = dquery[at * BLK : (at + 1) * BLK]

    for target in (own_ref, *send_refs):
        for side in range(2):
            target[:, columns[side]] = jnp.zeros((target.shape[0], HEAD_SIZE), target.dtype)
    for slot in range(act_total):
        steps = info_ref[slot]
        row = pl.multiple_of(info_ref[act_total + slot] * BLK, BLK)
        rows = slice(slot * BLK, (slot + 1) * BLK)
        for step, target in enumerate((own_ref, *send_refs)):

            @pl.when(steps == step)
            def _():
                target[pl.ds(row, BLK), columns[0]] = dk_scr[rows, :].astype(target.dtype)
                target[pl.ds(row, BLK), columns[1]] = dv_scr[rows, :].astype(target.dtype)


def attend(info, queries, cotangent, kv_steps, chunk, heads, group, act_total, dq_so_far):
    seq_count = len(kv_steps)
    tok_dev, width = kv_steps[0].shape
    qwidth = queries.shape[2]
    group_width = group * HEAD_SIZE
    q_spec = pl.BlockSpec((None, tok_dev, group_width), lambda i: (0, 0, chunk * heads + i))
    kv_specs = [
        pl.BlockSpec((tok_dev, HEAD_SIZE), lambda i: (0, i)),
        pl.BlockSpec((tok_dev, HEAD_SIZE), lambda i: (0, heads + i)),
    ]
    whole_spec = pl.BlockSpec((tok_dev, width), lambda i: (0, 0))
    sizes = (act_total, tok_dev // BLK, seq_count, group, dq_so_far is not None)
    operands = [info, queries, cotangent, *[kv for kv in kv_steps for _ in range(2)]]
    in_specs = [smem(), q_spec, q_spec] + kv_specs * seq_count
    aliases = {}
    if dq_so_far is not None:
        aliases = {len(operands): 0}
        operands.append(dq_so_far)
        in_specs.append(pl.BlockSpec(memory_space=pl.ANY))
    outs = pl.pallas_call(
        functools.partial(attend_kernel, sizes),
        grid=(heads,),
        out_shape=[
            jax.ShapeDtypeStruct((1, tok_dev, qwidth), jnp.bfloat16),
            jax.ShapeDtypeStruct((tok_dev, width), jnp.float32),
            *[jax.ShapeDtypeStruct((tok_dev, width), jnp.bfloat16) for _ in range(seq_count - 1)],
        ],
        in_specs=in_specs,
        out_specs=[q_spec] + [whole_spec] * seq_count,
        scratch_shapes=[pltpu.VMEM((act_total * BLK, HEAD_SIZE), jnp.bfloat16)] * 2
        + [pltpu.VMEM((act_total * BLK, HEAD_SIZE), jnp.float32)] * 2,
        input_output_aliases=aliases,
        compiler_params=pltpu.CompilerParams(vmem_limit_bytes=60 * 1024 * 1024),
        cost_estimate=lasting(9),
        name="attend",
    )(*operands)
    return outs[0], outs[1], outs[2:]


def token_kernel(tables, indices, rank_ref, *refs):
    out_ref = refs[-1]
    dkv_refs, refs = refs[: len(tables)], refs[len(tables) : -1]
    width = dkv_refs[0].shape[1] // 2
    count = len(tables[0])
    rows = out_ref.shape[-1] if len(out_ref.shape) == 3 else out_ref.shape[1] // count
    for at in range(count):
        owner = rank_ref[1] ^ at
        total = None
        for dkv_ref, table, index in zip(dkv_refs, tables, indices):
            arrays = [refs[number] for number in index]
            for side in range(2):
                term = dot(
                    dkv_ref[:, side * width : (side + 1) * width], side_of(table, arrays, at, side), 1, 1
                )
                total = term if total is None else total + term
        if len(out_ref.shape) == 3:
            out_ref[owner] = total.astype(out_ref.dtype)
        else:
            out_ref[:, pl.ds(pl.multiple_of(owner * rows, 128), rows)] = total.astype(out_ref.dtype)


def token_grads(rank, dkvs, weight_pieces, rows):
    flat, indices = [], []
    for arrays, _ in weight_pieces:
        index = []
        for array in arrays:
            known = [at for at, other in enumerate(flat) if other is array]
            if not known:
                known = [len(flat)]
                flat.append(array)
            index.append(known[0])
        indices.append(tuple(index))
    tables = tuple(table for _, table in weight_pieces)
    count = lax.axis_size("dp")
    tok_dev = dkvs[0].shape[0]
    flat_out = rows % 128 == 0
    shape = (tok_dev, count * rows) if flat_out else (count, tok_dev, rows)
    out = pl.pallas_call(
        functools.partial(token_kernel, tables, tuple(indices)),
        out_shape=jax.ShapeDtypeStruct(shape, jnp.bfloat16),
        in_specs=[smem()] + [vmem()] * (len(dkvs) + len(flat)),
        out_specs=vmem(),
        compiler_params=params(),
        cost_estimate=lasting(8),
        name="token_grads",
    )(rank, *dkvs, *flat)
    return out if flat_out else jnp.concatenate(list(out), axis=1)


def weight_kernel(dests, pieces_total, has_before, rank_ref, *refs):
    x_refs, refs = refs[:PARTS], refs[PARTS:]
    count = x_refs[0].shape[0]
    height = x_refs[0].shape[1] * PARTS
    pieces, refs = refs[:pieces_total], refs[pieces_total:]
    out_refs = refs[len(refs) // 2 :] if has_before else refs
    column, width = out_refs[0].shape[1], pieces[0].shape[1] // 2
    totals = [None, None]
    for at in range(count):
        rows = rows_of(x_refs, rank_ref[1] ^ at)
        for side in range(2):
            if pieces_total == count:
                piece, start = pieces[at], 0
            else:
                piece, start = pieces[at % 2], at // 2 * height
            term = dot(rows, piece[start : start + height, side * width : (side + 1) * width], 0, 0)
            totals[side] = term if totals[side] is None else totals[side] + term
    for at, out_ref in enumerate(out_refs):
        if has_before:
            out_ref[...] = refs[at][...]
        for dest, side, offset in dests:

            @pl.when(rank_ref[0] ^ at == dest)
            def _():
                out_ref[...] = totals[side][:, offset : offset + column].astype(out_ref.dtype)


def weight_terms(rank, x_all, pieces, dests, column, before):
    seq_count = lax.axis_size("seq")
    rows = x_all[0].shape[2]
    operands = [*x_all, *pieces, *before]
    return pl.pallas_call(
        functools.partial(weight_kernel, dests, len(pieces), bool(before)),
        out_shape=[jax.ShapeDtypeStruct((rows, column), jnp.float32)]
        + [jax.ShapeDtypeStruct((rows, column), jnp.bfloat16)] * (seq_count - 1),
        in_specs=[smem()] + [vmem()] * len(operands),
        out_specs=[vmem()] * seq_count,
        compiler_params=params(),
        cost_estimate=lasting(4),
        name="weight_grad",
    )(rank, *operands)


def body(tokens, queries, cotangent, kv_weight, active):
    seq_count, dp_count = lax.axis_size("seq"), lax.axis_size("dp")
    seq_rank, dp_rank = lax.axis_index("seq"), lax.axis_index("dp")
    tok_dev, model = tokens.shape[1], tokens.shape[2]
    qwidth, kvwidth = queries.shape[2], kv_weight.shape[1]
    rows = kv_weight.shape[0]
    act_total = active.shape[1]
    kv_heads = kvwidth // (2 * HEAD_SIZE)
    group = qwidth // (HEAD_SIZE * kv_heads)
    heads = kv_heads // CHUNKS
    width = heads * HEAD_SIZE
    blocks_dev = tok_dev // BLK
    column = kvwidth // seq_count

    block_ids = active[0]
    local_ids = seq_rank * blocks_dev + jnp.arange(blocks_dev, dtype=jnp.int32)
    match = (block_ids[None, :] == local_ids[:, None]).astype(jnp.int32)
    slot_rank = jnp.sum(match * jnp.arange(1, act_total + 1, dtype=jnp.int32)[None, :], axis=1) - 1
    info = jnp.concatenate(
        [seq_rank - block_ids // blocks_dev, block_ids % blocks_dev, slot_rank]
    ).astype(jnp.int32)
    rank = jnp.stack([seq_rank, dp_rank]).astype(jnp.int32)

    x_by_owner = split_columns(tokens, dp_count)

    dq = None
    dkvs, terms = [], []
    shards = []
    for chunk in range(CHUNKS):
        key_at, value_at = chunk * width, kvwidth // 2 + chunk * width
        shards.append(
            jnp.concatenate(
                [kv_weight[:, key_at : key_at + width], kv_weight[:, value_at : value_at + width]], axis=1
            )
        )
    weight_pieces, keyvals, weight_gates = gather_weights(
        shards, x_by_owner, lambda pieces: relay(project(rank, x_by_owner, pieces))
    )
    arrivals, keyvals = keyvals, [steps[0] for steps in keyvals]
    for chunk in range(1, CHUNKS):
        keyvals.append(project(rank, x_by_owner, weight_pieces[chunk]))
        arrivals[-1] = (finish_relay if chunk == 1 else finish)(arrivals[-1], keyvals[-1])
        arrivals.append(spread(keyvals[-1]))
    arrivals = [steps[1:] for steps in [*arrivals[:-1], finish(arrivals[-1])]]
    x_all, gates = [], weight_gates
    for part in x_by_owner:
        part = lax.all_to_all(after(part, *gates), "dp", split_axis=0, concat_axis=0, tiled=True)
        x_all.append(part)
        gates = (part,)

    backs, owns = [], []
    gates, waits, later = (keyvals[-1],), tuple(arrivals[-1][1:2]), ()
    for chunk in range(CHUNKS):
        kv_steps = [keyvals[chunk]] + arrivals[chunk]
        dq, own, sends = attend(
            after(info, *gates), queries, cotangent, kv_steps, chunk, heads, group, act_total, dq
        )
        if chunk < CHUNKS - 1 or seq_count > 4:
            arrived, back = collect(sends, waits, later)
        else:
            back = [moved(after(sends[step - 1], *waits), "seq", -step) for step in range(seq_count - 1, 0, -1)]
            arrived = ()
        backs.append(back)
        owns.append(own)
        gates, waits, later = (*arrived, *x_all), tuple(back), ()
    gates, sums = (owns[-1],), ()
    for chunk in range(CHUNKS):
        total = after(owns[chunk], *gates)
        for part in backs[chunk]:
            total = total + part.astype(jnp.float32)
        dkvs.append(total.astype(jnp.bfloat16))
        if chunk < CHUNKS - 1 or lax.axis_size("dp") > 8:
            dkv_pieces = gather_doubling(dkvs[chunk], backs[-1][:1], backs[-1][1:])
        else:
            dkv_pieces = gather_direct(dkvs[chunk], *sums[:1])
        dests = []
        for side in range(2):
            start = side * (kvwidth // 2) + chunk * width
            for offset in range(0, width, column):
                dests.append(((start + offset) // column, side, offset))
        sums = weight_terms(rank, x_all, dkv_pieces, dests, column, sums)
        gates = ()
    gates = (sums[0],)
    terms = [sums[0]]
    for at, send in enumerate(sums[1:]):
        terms.append(exchange(send, "seq", at + 1).astype(jnp.float32))
    weight_grad = functools.reduce(lambda a, b: a + b, terms)
    token_grad = token_grads(after(rank, *gates), dkvs, weight_pieces, rows)
    return (dq, token_grad[None], weight_grad)


def solution(mesh):
    in_specs = (
        P("dp", "seq", None),
        P("dp", "seq", None),
        P("dp", "seq", None),
        P("dp", None),
        P("dp", None),
    )
    out_specs = (P("dp", "seq", None), P("dp", "seq", None), P("dp", "seq"))
    return jax.shard_map(body, mesh=mesh, in_specs=in_specs, out_specs=out_specs, check_vma=False)
```

```python
import functools
import math

import jax
import jax.numpy as jnp
from jax import lax
from jax.experimental import pallas as pl
from jax.experimental.pallas import tpu as pltpu
from jax.sharding import PartitionSpec as P

HEAD_SIZE = 128
BLK = 128
CHUNKS = 2
PARTS = 1
VMEM_BYTES = 24 * 1024 * 1024
MASKED = -1e30


def params():
    return pltpu.CompilerParams(vmem_limit_bytes=VMEM_BYTES)


def lasting(microseconds):
    return pl.CostEstimate(flops=4000000000 * microseconds, bytes_accessed=12000000 * microseconds, transcendentals=0)


def vmem():
    return pl.BlockSpec(memory_space=pltpu.VMEM)


def smem():
    return pl.BlockSpec(memory_space=pltpu.SMEM)


def dot(left, right, left_dim, right_dim):
    return lax.dot_general(
        left, right, (((left_dim,), (right_dim,)), ((), ())), preferred_element_type=jnp.float32
    )


def exchange(value, axis, mask):
    count = lax.axis_size(axis)
    return lax.ppermute(value, axis, [(i, i ^ mask) for i in range(count)])


def moved(value, axis, step, first=0):
    count = lax.axis_size(axis)
    pairs = [(i, i + step) for i in range(first, count) if 0 <= i + step < count]
    return lax.ppermute(value, axis, pairs)


def spread(value):
    count = lax.axis_size("seq")
    steps = [value] + [None] * (count - 1)
    for step in range(2, count, 2):
        steps[step] = moved(steps[step - 2], "seq", 2, step - 2)
    if count > 1:
        steps[1] = moved(value, "seq", 1)
    return steps


def relay(value):
    steps = [value]
    for step in range(1, lax.axis_size("seq")):
        steps.append(moved(steps[-1], "seq", 1, step - 1))
    return steps


def finish(steps, *gates):
    for step in range(3, len(steps), 2):
        steps[step] = moved(after(steps[step - 1], *gates), "seq", 1, step - 1)
    return steps


def added(left, right):
    return (left.astype(jnp.float32) + right.astype(jnp.float32)).astype(left.dtype)


def collect(sends, gates, later):
    count = lax.axis_size("seq")
    sends = [None, *sends]
    sends = [None] + [after(send, *gates) for send in sends[1:]]
    arrived = []
    for step in range(3, count, 2):
        arrived.append(moved(sends[step], "seq", -1, step))
        sends[step - 1] = added(sends[step - 1], arrived[-1])
    if len(sends) > 2:
        sends[2] = after(sends[2], *later)
    for step in range((count - 1) // 2 * 2, 2, -2):
        sends[step - 2] = added(sends[step - 2], moved(sends[step], "seq", -2, step))
    return arrived, [moved(sends[step], "seq", -step, step) for step in (1, 2) if step < count]


def gather_direct(own, *gates):
    count = lax.axis_size("dp")
    pieces = [own] + [None] * (count - 1)
    for mask in range(2, count, 2):
        pieces[mask] = exchange(own, "dp", mask)
    for mask in range(0, count, 2):
        pieces[mask + 1] = exchange(after(pieces[mask], *gates), "dp", 1)
    return pieces


def gather_doubling(own, second, last):
    bit, stack = 2, own
    while bit < lax.axis_size("dp"):
        stack = jnp.concatenate([stack, exchange(stack, "dp", bit)], axis=0)
        if bit == 2:
            stack = after(stack, *second)
        bit *= 2
    return [stack, exchange(after(stack, *last), "dp", 1)]


def after(value, *others):
    return lax.optimization_barrier((value, others))[0]


def side_of(table, refs, at, side):
    array, start, width = table[at][side]
    return refs[array][:, start : start + width]


def whole_table(count, width):
    return tuple(((at, 0, width), (at, width, width)) for at in range(count))


def halves_kernel(near_ref, far_ref, left_ref, right_ref, *, near_start, far_start):
    width = left_ref.shape[1]
    left_ref[...] = near_ref[:, near_start : near_start + width]
    right_ref[...] = far_ref[:, far_start : far_start + width]


def halves(near, far, near_start, far_start):
    shape = jax.ShapeDtypeStruct((near.shape[0], near.shape[1] // 2), near.dtype)
    return pl.pallas_call(
        functools.partial(halves_kernel, near_start=near_start, far_start=far_start),
        out_shape=[shape, shape],
        in_specs=[vmem()] * 2,
        out_specs=[vmem()] * 2,
        compiler_params=params(),
        cost_estimate=lasting(1),
        name="halves",
    )(near, far)


def gather_weights(shards, behind, use_first):
    count = lax.axis_size("dp")
    width = shards[0].shape[1] // 2
    if count != 8 or len(shards) != 2:
        result = []
        for shard in shards:
            pieces = gather_direct(shard)
            result.append((pieces, whole_table(count, width)))
        return result, [use_first(result[0])], pieces[-1:]
    first, second = shards
    table = []
    for entry in [((0, 0), (0, 1)), ((1, 0), (1, 1)), ((2, 0), (2, 1)), ((3, 0), (4, 0))]:
        for core in range(2):
            table.append(tuple((array + core * 5, part * width, width) for array, part in entry))
    table = tuple(table)

    def near_of(own, *gates):
        from_x, from_y = after((exchange(own, "dp", 2), exchange(own, "dp", 4)), *gates)
        to_y, to_x = halves(from_x, from_y, 0, width)
        return [from_x, from_y, exchange(to_y, "dp", 4), exchange(to_x, "dp", 2)]

    def with_core(own, own_core, others):
        cores = [exchange(part, "dp", 1) for part in others]
        return [own, *others, own_core, *cores], table

    others = near_of(first, *behind, second)
    pieces = [with_core(first, exchange(first, "dp", 1), others)]
    used = use_first(pieces[0])
    hops = list(used[1:]) + [used[0]] * 3
    second_core = exchange(after(second, used[0]), "dp", 1)
    others = near_of(after(second, *others[2:]), hops[0], second_core)
    pieces.append(with_core(second, second_core, others))
    return pieces, [used], hops[1:2]


def split_kernel(x_ref, *out_refs):
    for at, out_ref in enumerate(out_refs):
        height = out_ref.shape[0]
        out_ref[...] = x_ref[at * height : (at + 1) * height]


def split_columns(tokens, count):
    tok_dev, model = tokens.shape[1:]
    rows, height = model // count, tok_dev // PARTS
    if rows % 128:
        return [
            jnp.stack([tokens[0, part * height : (part + 1) * height, at * rows : (at + 1) * rows] for at in range(count)])
            for part in range(PARTS)
        ]
    return pl.pallas_call(
        split_kernel,
        grid=(count,),
        out_shape=[jax.ShapeDtypeStruct((count, height, rows), tokens.dtype)] * PARTS,
        in_specs=[pl.BlockSpec((None, tok_dev, rows), lambda at: (0, 0, at))],
        out_specs=[pl.BlockSpec((None, height, rows), lambda at: (at, 0, 0))] * PARTS,
        compiler_params=params(),
        cost_estimate=lasting(3),
        name="split_columns",
    )(tokens)


def rows_of(x_refs, owner):
    return jnp.concatenate([x_ref[owner] for x_ref in x_refs], axis=0)


def project_kernel(table, rank_ref, *refs):
    x_refs, refs, out_ref = refs[:PARTS], refs[PARTS:-1], refs[-1]
    width = out_ref.shape[1] // 2
    totals = [None, None]
    for at in range(len(table)):
        rows = rows_of(x_refs, rank_ref[1] ^ at)
        for side in range(2):
            term = dot(rows, side_of(table, refs, at, side), 1, 0)
            totals[side] = term if totals[side] is None else totals[side] + term
    for side in range(2):
        out_ref[:, side * width : (side + 1) * width] = totals[side].astype(out_ref.dtype)


def project(rank, x_by_owner, pieces):
    arrays, table = pieces
    tok_dev, width = x_by_owner[0].shape[1] * PARTS, table[0][0][2] * 2
    return pl.pallas_call(
        functools.partial(project_kernel, table),
        out_shape=jax.ShapeDtypeStruct((tok_dev, width), jnp.bfloat16),
        in_specs=[smem()] + [vmem()] * (PARTS + len(arrays)),
        out_specs=vmem(),
        compiler_params=params(),
        cost_estimate=lasting(4),
        name="project",
    )(rank, *x_by_owner, *arrays)


def attend_kernel(sizes, info_ref, q_ref, g_ref, *refs):
    act_total, blocks_dev, seq_count, group, has_alias = sizes
    kv_refs = refs[: 2 * seq_count]
    refs = refs[2 * seq_count + (1 if has_alias else 0) :]
    dq_ref, own_ref = refs[0], refs[1]
    send_refs = refs[2 : 1 + seq_count]
    k_scr, v_scr, dk_scr, dv_scr = refs[1 + seq_count :]
    head = pl.program_id(0)
    width = own_ref.shape[1] // 2
    scale = 1.0 / math.sqrt(HEAD_SIZE)
    columns = [pl.ds(pl.multiple_of(side * width + head * HEAD_SIZE, HEAD_SIZE), HEAD_SIZE) for side in range(2)]
    dk_scr[...] = jnp.zeros_like(dk_scr)
    dv_scr[...] = jnp.zeros_like(dv_scr)
    for slot in range(act_total):
        steps = info_ref[slot]
        row = pl.multiple_of(info_ref[act_total + slot] * BLK, BLK)
        rows = slice(slot * BLK, (slot + 1) * BLK)

        @pl.when(steps < 0)
        def _():
            k_scr[rows, :] = jnp.zeros((BLK, HEAD_SIZE), k_scr.dtype)
            v_scr[rows, :] = jnp.zeros((BLK, HEAD_SIZE), v_scr.dtype)

        for step in range(seq_count):

            @pl.when(steps == step)
            def _():
                k_scr[rows, :] = kv_refs[2 * step][pl.ds(row, BLK), :]
                v_scr[rows, :] = kv_refs[2 * step + 1][pl.ds(row, BLK), :]

    def attend_block(rows, slots):
        span = slots * BLK
        keys, values = k_scr[:span, :], v_scr[:span, :]
        query, gradient = (
            jnp.concatenate([ref[rows, at * HEAD_SIZE : (at + 1) * HEAD_SIZE] for at in range(group)], axis=0)
            for ref in (q_ref, g_ref)
        )
        scores = dot(keys, query, 1, 1)
        last = scores[span - BLK :]
        key_pos = lax.broadcasted_iota(jnp.int32, last.shape, 0)
        query_pos = lax.broadcasted_iota(jnp.int32, last.shape, 1) & (BLK - 1)
        last = jnp.where(key_pos <= query_pos, last, MASKED)
        scores = last if slots == 1 else jnp.concatenate([scores[: span - BLK], last], axis=0)
        top = jnp.max(scores, axis=0, keepdims=True)
        exponent = jnp.exp2((scores - top) * (scale * math.log2(math.e)))
        probs = exponent * (1.0 / jnp.sum(exponent, axis=0, keepdims=True))
        dprobs = dot(values, gradient, 1, 1)
        delta = jnp.sum(probs * dprobs, axis=0, keepdims=True)
        dscores = (probs * (dprobs - delta)).astype(jnp.bfloat16)
        dk_scr[:span, :] += dot(dscores, query, 1, 0)
        dv_scr[:span, :] += dot(probs.astype(jnp.bfloat16), gradient, 1, 0)
        dquery = (dot(keys, dscores, 0, 0) * scale).T.astype(dq_ref.dtype)
        for at in range(group):
            dq_ref[rows, at * HEAD_SIZE : (at + 1) * HEAD_SIZE] = dquery[at * BLK : (at + 1) * BLK]

    @pl.loop(0, blocks_dev)
    def _(block):
        rank = info_ref[2 * act_total + block]
        rows = pl.ds(pl.multiple_of(block * BLK, BLK), BLK)

        @pl.when(rank < 0)
        def _():
            dq_ref[rows, :] = jnp.zeros((BLK, group * HEAD_SIZE), dq_ref.dtype)

        for slots in range(1, act_total + 1):

            @pl.when(rank == slots - 1)
            def _():
                attend_block(rows, slots)

    for target in (own_ref, *send_refs):
        for side in range(2):
            target[:, columns[side]] = jnp.zeros((target.shape[0], HEAD_SIZE), target.dtype)
    for slot in range(act_total):
        steps = info_ref[slot]
        row = pl.multiple_of(info_ref[act_total + slot] * BLK, BLK)
        rows = slice(slot * BLK, (slot + 1) * BLK)
        for step, target in enumerate((own_ref, *send_refs)):

            @pl.when(steps == step)
            def _():
                target[pl.ds(row, BLK), columns[0]] = (dk_scr[rows, :] * scale).astype(target.dtype)
                target[pl.ds(row, BLK), columns[1]] = dv_scr[rows, :].astype(target.dtype)


def attend(info, queries, cotangent, kv_steps, chunk, heads, group, act_total, dq_so_far):
    seq_count = len(kv_steps)
    tok_dev, width = kv_steps[0].shape
    qwidth = queries.shape[2]
    group_width = group * HEAD_SIZE
    q_spec = pl.BlockSpec((None, tok_dev, group_width), lambda i: (0, 0, chunk * heads + i))
    kv_specs = [
        pl.BlockSpec((tok_dev, HEAD_SIZE), lambda i: (0, i)),
        pl.BlockSpec((tok_dev, HEAD_SIZE), lambda i: (0, heads + i)),
    ]
    whole_spec = pl.BlockSpec((tok_dev, width), lambda i: (0, 0))
    sizes = (act_total, tok_dev // BLK, seq_count, group, dq_so_far is not None)
    operands = [info, queries, cotangent, *[kv for kv in kv_steps for _ in range(2)]]
    in_specs = [smem(), q_spec, q_spec] + kv_specs * seq_count
    aliases = {}
    if dq_so_far is not None:
        aliases = {len(operands): 0}
        operands.append(dq_so_far)
        in_specs.append(pl.BlockSpec(memory_space=pl.ANY))
    outs = pl.pallas_call(
        functools.partial(attend_kernel, sizes),
        grid=(heads,),
        out_shape=[
            jax.ShapeDtypeStruct((1, tok_dev, qwidth), jnp.bfloat16),
            jax.ShapeDtypeStruct((tok_dev, width), jnp.float32),
            *[jax.ShapeDtypeStruct((tok_dev, width), jnp.bfloat16) for _ in range(seq_count - 1)],
        ],
        in_specs=in_specs,
        out_specs=[q_spec] + [whole_spec] * seq_count,
        scratch_shapes=[pltpu.VMEM((act_total * BLK, HEAD_SIZE), jnp.bfloat16)] * 2
        + [pltpu.VMEM((act_total * BLK, HEAD_SIZE), jnp.float32)] * 2,
        input_output_aliases=aliases,
        compiler_params=pltpu.CompilerParams(vmem_limit_bytes=60 * 1024 * 1024),
        cost_estimate=lasting(2 if chunk == 1 else 9),
        name="attend",
    )(*operands)
    return outs[0], outs[1], outs[2:]


def token_kernel(tables, indices, rank_ref, *refs):
    out_ref = refs[-1]
    dkv_refs, refs = refs[: len(tables)], refs[len(tables) : -1]
    width = dkv_refs[0].shape[1] // 2
    count = len(tables[0])
    rows = out_ref.shape[-1] if len(out_ref.shape) == 3 else out_ref.shape[1] // count
    for at in range(count):
        owner = rank_ref[1] ^ at
        total = None
        for dkv_ref, table, index in zip(dkv_refs, tables, indices):
            arrays = [refs[number] for number in index]
            for side in range(2):
                term = dot(
                    dkv_ref[:, side * width : (side + 1) * width], side_of(table, arrays, at, side), 1, 1
                )
                total = term if total is None else total + term
        if len(out_ref.shape) == 3:
            out_ref[owner] = total.astype(out_ref.dtype)
        else:
            out_ref[:, pl.ds(pl.multiple_of(owner * rows, 128), rows)] = total.astype(out_ref.dtype)


def token_grads(rank, dkvs, weight_pieces, rows):
    flat, indices = [], []
    for arrays, _ in weight_pieces:
        index = []
        for array in arrays:
            known = [at for at, other in enumerate(flat) if other is array]
            if not known:
                known = [len(flat)]
                flat.append(array)
            index.append(known[0])
        indices.append(tuple(index))
    tables = tuple(table for _, table in weight_pieces)
    count = lax.axis_size("dp")
    tok_dev = dkvs[0].shape[0]
    flat_out = rows % 128 == 0
    shape = (tok_dev, count * rows) if flat_out else (count, tok_dev, rows)
    out = pl.pallas_call(
        functools.partial(token_kernel, tables, tuple(indices)),
        out_shape=jax.ShapeDtypeStruct(shape, jnp.bfloat16),
        in_specs=[smem()] + [vmem()] * (len(dkvs) + len(flat)),
        out_specs=vmem(),
        compiler_params=params(),
        cost_estimate=lasting(8),
        name="token_grads",
    )(rank, *dkvs, *flat)
    return out if flat_out else jnp.concatenate(list(out), axis=1)


def weight_kernel(dests, pieces_total, has_before, rank_ref, *refs):
    x_refs, refs = refs[:PARTS], refs[PARTS:]
    count = x_refs[0].shape[0]
    height = x_refs[0].shape[1] * PARTS
    pieces, refs = refs[:pieces_total], refs[pieces_total:]
    out_refs = refs[len(refs) // 2 :] if has_before else refs
    column, width = out_refs[0].shape[1], pieces[0].shape[1] // 2
    totals = [None, None]
    for at in range(count):
        rows = rows_of(x_refs, rank_ref[1] ^ at)
        for side in range(2):
            if pieces_total == count:
                piece, start = pieces[at], 0
            else:
                piece, start = pieces[at % 2], at // 2 * height
            term = dot(rows, piece[start : start + height, side * width : (side + 1) * width], 0, 0)
            totals[side] = term if totals[side] is None else totals[side] + term
    for at, out_ref in enumerate(out_refs):
        if has_before:
            out_ref[...] = refs[at][...]
        for dest, side, offset in dests:

            @pl.when(rank_ref[0] ^ at == dest)
            def _():
                out_ref[...] = totals[side][:, offset : offset + column].astype(out_ref.dtype)


def weight_terms(rank, x_all, pieces, dests, column, before):
    seq_count = lax.axis_size("seq")
    rows = x_all[0].shape[2]
    operands = [*x_all, *pieces, *before]
    return pl.pallas_call(
        functools.partial(weight_kernel, dests, len(pieces), bool(before)),
        out_shape=[jax.ShapeDtypeStruct((rows, column), jnp.float32)]
        + [jax.ShapeDtypeStruct((rows, column), jnp.bfloat16)] * (seq_count - 1),
        in_specs=[smem()] + [vmem()] * len(operands),
        out_specs=[vmem()] * seq_count,
        compiler_params=params(),
        cost_estimate=lasting(4),
        name="weight_grad",
    )(rank, *operands)


def body(tokens, queries, cotangent, kv_weight, active):
    seq_count, dp_count = lax.axis_size("seq"), lax.axis_size("dp")
    seq_rank, dp_rank = lax.axis_index("seq"), lax.axis_index("dp")
    tok_dev, model = tokens.shape[1], tokens.shape[2]
    qwidth, kvwidth = queries.shape[2], kv_weight.shape[1]
    rows = kv_weight.shape[0]
    act_total = active.shape[1]
    kv_heads = kvwidth // (2 * HEAD_SIZE)
    group = qwidth // (HEAD_SIZE * kv_heads)
    heads = kv_heads // CHUNKS
    width = heads * HEAD_SIZE
    blocks_dev = tok_dev // BLK
    column = kvwidth // seq_count

    block_ids = active[0]
    local_ids = seq_rank * blocks_dev + jnp.arange(blocks_dev, dtype=jnp.int32)
    match = (block_ids[None, :] == local_ids[:, None]).astype(jnp.int32)
    slot_rank = jnp.sum(match * jnp.arange(1, act_total + 1, dtype=jnp.int32)[None, :], axis=1) - 1
    info = jnp.concatenate(
        [seq_rank - block_ids // blocks_dev, block_ids % blocks_dev, slot_rank]
    ).astype(jnp.int32)
    rank = jnp.stack([seq_rank, dp_rank]).astype(jnp.int32)

    x_by_owner = split_columns(tokens, dp_count)

    dq = None
    dkvs, terms = [], []
    shards = []
    for chunk in range(CHUNKS):
        key_at, value_at = chunk * width, kvwidth // 2 + chunk * width
        shards.append(
            jnp.concatenate(
                [kv_weight[:, key_at : key_at + width], kv_weight[:, value_at : value_at + width]], axis=1
            )
        )
    weight_pieces, keyvals, weight_gates = gather_weights(
        shards, x_by_owner, lambda pieces: relay(project(rank, x_by_owner, pieces))
    )
    arrivals, keyvals = keyvals, [steps[0] for steps in keyvals]
    for chunk in range(1, CHUNKS):
        keyvals.append(project(rank, x_by_owner, weight_pieces[chunk]))
        arrivals[-1] = arrivals[-1] if chunk == 1 else finish(arrivals[-1], keyvals[-1])
        arrivals.append(spread(keyvals[-1]))
    arrivals = [steps[1:] for steps in [*arrivals[:-1], finish(arrivals[-1])]]
    x_all, gates = [], (keyvals[-1],)
    for part in x_by_owner:
        part = lax.all_to_all(after(part, *gates), "dp", split_axis=0, concat_axis=0, tiled=True)
        x_all.append(part)
        gates = (part,)

    backs, owns = [], []
    gates, waits, later = (keyvals[-1],), tuple(arrivals[-1][1:2]), ()
    for chunk in range(CHUNKS):
        kv_steps = [keyvals[chunk]] + arrivals[chunk]
        dq, own, sends = attend(
            after(info, *gates), queries, cotangent, kv_steps, chunk, heads, group, act_total, dq
        )
        if chunk < CHUNKS - 1 or seq_count > 4:
            arrived, back = collect(sends, waits, later)
        else:
            back = [moved(after(sends[step - 1], *waits), "seq", -step) for step in range(seq_count - 1, 0, -1)]
            arrived = ()
        backs.append(back)
        owns.append(own)
        gates, waits, later = tuple(arrived), (*back, *x_all), ()
    gates, sums = (owns[-1],), ()
    for chunk in range(CHUNKS):
        total = after(owns[chunk], *gates)
        for part in backs[chunk]:
            total = total + part.astype(jnp.float32)
        dkvs.append(total.astype(jnp.bfloat16))
        if chunk < CHUNKS - 1 or lax.axis_size("dp") > 8:
            dkv_pieces = gather_doubling(dkvs[chunk], backs[-1][:1], backs[-1][1:])
        else:
            dkv_pieces = gather_direct(dkvs[chunk], *sums[:1])
        dests = []
        for side in range(2):
            start = side * (kvwidth // 2) + chunk * width
            for offset in range(0, width, column):
                dests.append(((start + offset) // column, side, offset))
        sums = weight_terms(rank, x_all, dkv_pieces, dests, column, sums)
        gates = ()
    gates = (sums[0],)
    terms = [sums[0]]
    for at, send in enumerate(sums[1:]):
        terms.append(exchange(send, "seq", at + 1).astype(jnp.float32))
    weight_grad = functools.reduce(lambda a, b: a + b, terms)
    token_grad = token_grads(after(rank, *gates), dkvs, weight_pieces, rows)
    return (dq, token_grad[None], weight_grad)


def solution(mesh):
    in_specs = (
        P("dp", "seq", None),
        P("dp", "seq", None),
        P("dp", "seq", None),
        P("dp", None),
        P("dp", None),
    )
    out_specs = (P("dp", "seq", None), P("dp", "seq", None), P("dp", "seq"))
    return jax.shard_map(body, mesh=mesh, in_specs=in_specs, out_specs=out_specs, check_vma=False)
```

```python
import functools
import math

import jax
import jax.numpy as jnp
from jax import lax
from jax.experimental import pallas as pl
from jax.experimental.pallas import tpu as pltpu
from jax.sharding import PartitionSpec as P

HEAD_SIZE = 128
BLK = 128
CHUNKS = 2
PARTS = 1
VMEM_BYTES = 24 * 1024 * 1024
MASKED = -1e30


def params():
    return pltpu.CompilerParams(vmem_limit_bytes=VMEM_BYTES)


def lasting(microseconds):
    return pl.CostEstimate(flops=4000000000 * microseconds, bytes_accessed=12000000 * microseconds, transcendentals=0)


def vmem():
    return pl.BlockSpec(memory_space=pltpu.VMEM)


def smem():
    return pl.BlockSpec(memory_space=pltpu.SMEM)


def dot(left, right, left_dim, right_dim):
    return lax.dot_general(
        left, right, (((left_dim,), (right_dim,)), ((), ())), preferred_element_type=jnp.float32
    )


def exchange(value, axis, mask):
    count = lax.axis_size(axis)
    return lax.ppermute(value, axis, [(i, i ^ mask) for i in range(count)])


def moved(value, axis, step, first=0):
    count = lax.axis_size(axis)
    pairs = [(i, i + step) for i in range(first, count) if 0 <= i + step < count]
    return lax.ppermute(value, axis, pairs)


def spread(value):
    count = lax.axis_size("seq")
    steps = [value] + [None] * (count - 1)
    for step in range(2, count, 2):
        steps[step] = moved(steps[step - 2], "seq", 2, step - 2)
    if count > 1:
        steps[1] = moved(value, "seq", 1)
    return steps


def relay(value):
    steps = [value]
    for step in range(1, lax.axis_size("seq")):
        steps.append(moved(steps[-1], "seq", 1, step - 1))
    return steps


def finish(steps, *gates):
    for step in range(3, len(steps), 2):
        steps[step] = moved(after(steps[step - 1], *gates), "seq", 1, step - 1)
    return steps


def added(left, right):
    return (left.astype(jnp.float32) + right.astype(jnp.float32)).astype(left.dtype)


def collect(sends, gates, later):
    count = lax.axis_size("seq")
    sends = [None, *sends]
    sends = [None] + [after(send, *gates) for send in sends[1:]]
    arrived = []
    for step in range(3, count, 2):
        arrived.append(moved(sends[step], "seq", -1, step))
        sends[step - 1] = added(sends[step - 1], arrived[-1])
    if len(sends) > 2:
        sends[2] = after(sends[2], *later)
    for step in range((count - 1) // 2 * 2, 2, -2):
        sends[step - 2] = added(sends[step - 2], moved(sends[step], "seq", -2, step))
    return arrived, [moved(sends[step], "seq", -step, step) for step in (1, 2) if step < count]


def gather_direct(own, *gates):
    count = lax.axis_size("dp")
    pieces = [own] + [None] * (count - 1)
    for mask in range(2, count, 2):
        pieces[mask] = exchange(own, "dp", mask)
    for mask in range(0, count, 2):
        pieces[mask + 1] = exchange(after(pieces[mask], *gates), "dp", 1)
    return pieces


def gather_doubling(own, second, last):
    bit, stack = 2, own
    while bit < lax.axis_size("dp"):
        stack = jnp.concatenate([stack, exchange(stack, "dp", bit)], axis=0)
        if bit == 2:
            stack = after(stack, *second)
        bit *= 2
    return [stack, exchange(after(stack, *last), "dp", 1)]


def after(value, *others):
    return lax.optimization_barrier((value, others))[0]


def side_of(table, refs, at, side):
    array, start, width = table[at][side]
    return refs[array][:, start : start + width]


def whole_table(count, width):
    return tuple(((at, 0, width), (at, width, width)) for at in range(count))


def halves_kernel(near_ref, far_ref, left_ref, right_ref, *, near_start, far_start):
    width = left_ref.shape[1]
    left_ref[...] = near_ref[:, near_start : near_start + width]
    right_ref[...] = far_ref[:, far_start : far_start + width]


def halves(near, far, near_start, far_start):
    shape = jax.ShapeDtypeStruct((near.shape[0], near.shape[1] // 2), near.dtype)
    return pl.pallas_call(
        functools.partial(halves_kernel, near_start=near_start, far_start=far_start),
        out_shape=[shape, shape],
        in_specs=[vmem()] * 2,
        out_specs=[vmem()] * 2,
        compiler_params=params(),
        cost_estimate=lasting(1),
        name="halves",
    )(near, far)


def gather_weights(shards, behind, use_first):
    count = lax.axis_size("dp")
    width = shards[0].shape[1] // 2
    if count != 8 or len(shards) != 2:
        result = []
        for shard in shards:
            pieces = gather_direct(shard)
            result.append((pieces, whole_table(count, width)))
        return result, [use_first(result[0])], pieces[-1:]
    first, second = shards
    table = []
    for entry in [((0, 0), (0, 1)), ((1, 0), (1, 1)), ((2, 0), (2, 1)), ((3, 0), (4, 0))]:
        for core in range(2):
            table.append(tuple((array + core * 5, part * width, width) for array, part in entry))
    table = tuple(table)

    def near_of(own, *gates):
        from_x, from_y = after((exchange(own, "dp", 2), exchange(own, "dp", 4)), *gates)
        to_y, to_x = halves(from_x, from_y, 0, width)
        return [from_x, from_y, exchange(to_y, "dp", 4), exchange(to_x, "dp", 2)]

    def with_core(own, own_core, others):
        cores = [exchange(part, "dp", 1) for part in others]
        return [own, *others, own_core, *cores], table

    others = near_of(first, *behind, second)
    pieces = [with_core(first, exchange(first, "dp", 1), others)]
    used = use_first(pieces[0])
    hops = list(used[1:]) + [used[0]] * 3
    second_core = exchange(after(second, used[0]), "dp", 1)
    others = near_of(after(second, *others[2:]), hops[0], second_core)
    pieces.append(with_core(second, second_core, [*others[:2], *after(tuple(others[2:]), hops[1])]))
    return pieces, [used], hops[1:2]


def split_kernel(x_ref, *out_refs):
    for at, out_ref in enumerate(out_refs):
        height = out_ref.shape[0]
        out_ref[...] = x_ref[at * height : (at + 1) * height]


def split_columns(tokens, count):
    tok_dev, model = tokens.shape[1:]
    rows, height = model // count, tok_dev // PARTS
    if rows % 128:
        return [
            jnp.stack([tokens[0, part * height : (part + 1) * height, at * rows : (at + 1) * rows] for at in range(count)])
            for part in range(PARTS)
        ]
    return pl.pallas_call(
        split_kernel,
        grid=(count,),
        out_shape=[jax.ShapeDtypeStruct((count, height, rows), tokens.dtype)] * PARTS,
        in_specs=[pl.BlockSpec((None, tok_dev, rows), lambda at: (0, 0, at))],
        out_specs=[pl.BlockSpec((None, height, rows), lambda at: (at, 0, 0))] * PARTS,
        compiler_params=params(),
        cost_estimate=lasting(3),
        name="split_columns",
    )(tokens)


def rows_of(x_refs, owner):
    return jnp.concatenate([x_ref[owner] for x_ref in x_refs], axis=0)


def project_kernel(table, rank_ref, *refs):
    x_refs, refs, out_ref = refs[:PARTS], refs[PARTS:-1], refs[-1]
    width = out_ref.shape[1] // 2
    totals = [None, None]
    for at in range(len(table)):
        rows = rows_of(x_refs, rank_ref[1] ^ at)
        for side in range(2):
            term = dot(rows, side_of(table, refs, at, side), 1, 0)
            totals[side] = term if totals[side] is None else totals[side] + term
    for side in range(2):
        out_ref[:, side * width : (side + 1) * width] = totals[side].astype(out_ref.dtype)


def project(rank, x_by_owner, pieces):
    arrays, table = pieces
    tok_dev, width = x_by_owner[0].shape[1] * PARTS, table[0][0][2] * 2
    return pl.pallas_call(
        functools.partial(project_kernel, table),
        out_shape=jax.ShapeDtypeStruct((tok_dev, width), jnp.bfloat16),
        in_specs=[smem()] + [vmem()] * (PARTS + len(arrays)),
        out_specs=vmem(),
        compiler_params=params(),
        cost_estimate=lasting(4),
        name="project",
    )(rank, *x_by_owner, *arrays)


def attend_kernel(sizes, info_ref, q_ref, g_ref, *refs):
    act_total, blocks_dev, seq_count, group, has_alias = sizes
    kv_refs = refs[: 2 * seq_count]
    refs = refs[2 * seq_count + (1 if has_alias else 0) :]
    dq_ref, own_ref = refs[0], refs[1]
    send_refs = refs[2 : 1 + seq_count]
    k_scr, v_scr, dk_scr, dv_scr = refs[1 + seq_count :]
    head = pl.program_id(0)
    width = own_ref.shape[1] // 2
    scale = 1.0 / math.sqrt(HEAD_SIZE)
    columns = [pl.ds(pl.multiple_of(side * width + head * HEAD_SIZE, HEAD_SIZE), HEAD_SIZE) for side in range(2)]
    dk_scr[...] = jnp.zeros_like(dk_scr)
    dv_scr[...] = jnp.zeros_like(dv_scr)
    for slot in range(act_total):
        steps = info_ref[slot]
        row = pl.multiple_of(info_ref[act_total + slot] * BLK, BLK)
        rows = slice(slot * BLK, (slot + 1) * BLK)

        @pl.when(steps < 0)
        def _():
            k_scr[rows, :] = jnp.zeros((BLK, HEAD_SIZE), k_scr.dtype)
            v_scr[rows, :] = jnp.zeros((BLK, HEAD_SIZE), v_scr.dtype)

        for step in range(seq_count):

            @pl.when(steps == step)
            def _():
                k_scr[rows, :] = kv_refs[2 * step][pl.ds(row, BLK), :]
                v_scr[rows, :] = kv_refs[2 * step + 1][pl.ds(row, BLK), :]

    def attend_block(rows, slots):
        span = slots * BLK
        keys, values = k_scr[:span, :], v_scr[:span, :]
        query, gradient = (
            jnp.concatenate([ref[rows, at * HEAD_SIZE : (at + 1) * HEAD_SIZE] for at in range(group)], axis=0)
            for ref in (q_ref, g_ref)
        )
        scores = dot(keys, query, 1, 1)
        last = scores[span - BLK :]
        key_pos = lax.broadcasted_iota(jnp.int32, last.shape, 0)
        query_pos = lax.broadcasted_iota(jnp.int32, last.shape, 1) & (BLK - 1)
        last = jnp.where(key_pos <= query_pos, last, MASKED)
        scores = last if slots == 1 else jnp.concatenate([scores[: span - BLK], last], axis=0)
        top = jnp.max(scores, axis=0, keepdims=True)
        exponent = jnp.exp2((scores - top) * (scale * math.log2(math.e)))
        probs = exponent * (1.0 / jnp.sum(exponent, axis=0, keepdims=True))
        dprobs = dot(values, gradient, 1, 1)
        delta = jnp.sum(probs * dprobs, axis=0, keepdims=True)
        dscores = (probs * (dprobs - delta)).astype(jnp.bfloat16)
        dk_scr[:span, :] += dot(dscores, query, 1, 0)
        dv_scr[:span, :] += dot(probs.astype(jnp.bfloat16), gradient, 1, 0)
        dquery = (dot(keys, dscores, 0, 0) * scale).T.astype(dq_ref.dtype)
        for at in range(group):
            dq_ref[rows, at * HEAD_SIZE : (at + 1) * HEAD_SIZE] = dquery[at * BLK : (at + 1) * BLK]

    @pl.loop(0, blocks_dev)
    def _(block):
        rank = info_ref[2 * act_total + block]
        rows = pl.ds(pl.multiple_of(block * BLK, BLK), BLK)

        @pl.when(rank < 0)
        def _():
            dq_ref[rows, :] = jnp.zeros((BLK, group * HEAD_SIZE), dq_ref.dtype)

        for slots in range(1, act_total + 1):

            @pl.when(rank == slots - 1)
            def _():
                attend_block(rows, slots)

    for target in (own_ref, *send_refs):
        for side in range(2):
            target[:, columns[side]] = jnp.zeros((target.shape[0], HEAD_SIZE), target.dtype)
    for slot in range(act_total):
        steps = info_ref[slot]
        row = pl.multiple_of(info_ref[act_total + slot] * BLK, BLK)
        rows = slice(slot * BLK, (slot + 1) * BLK)
        for step, target in enumerate((own_ref, *send_refs)):

            @pl.when(steps == step)
            def _():
                target[pl.ds(row, BLK), columns[0]] = (dk_scr[rows, :] * scale).astype(target.dtype)
                target[pl.ds(row, BLK), columns[1]] = dv_scr[rows, :].astype(target.dtype)


def attend(info, queries, cotangent, kv_steps, chunk, heads, group, act_total, dq_so_far):
    seq_count = len(kv_steps)
    tok_dev, width = kv_steps[0].shape
    qwidth = queries.shape[2]
    group_width = group * HEAD_SIZE
    q_spec = pl.BlockSpec((None, tok_dev, group_width), lambda i: (0, 0, chunk * heads + i))
    kv_specs = [
        pl.BlockSpec((tok_dev, HEAD_SIZE), lambda i: (0, i)),
        pl.BlockSpec((tok_dev, HEAD_SIZE), lambda i: (0, heads + i)),
    ]
    whole_spec = pl.BlockSpec((tok_dev, width), lambda i: (0, 0))
    sizes = (act_total, tok_dev // BLK, seq_count, group, dq_so_far is not None)
    operands = [info, queries, cotangent, *[kv for kv in kv_steps for _ in range(2)]]
    in_specs = [smem(), q_spec, q_spec] + kv_specs * seq_count
    aliases = {}
    if dq_so_far is not None:
        aliases = {len(operands): 0}
        operands.append(dq_so_far)
        in_specs.append(pl.BlockSpec(memory_space=pl.ANY))
    outs = pl.pallas_call(
        functools.partial(attend_kernel, sizes),
        grid=(heads,),
        out_shape=[
            jax.ShapeDtypeStruct((1, tok_dev, qwidth), jnp.bfloat16),
            jax.ShapeDtypeStruct((tok_dev, width), jnp.float32),
            *[jax.ShapeDtypeStruct((tok_dev, width), jnp.bfloat16) for _ in range(seq_count - 1)],
        ],
        in_specs=in_specs,
        out_specs=[q_spec] + [whole_spec] * seq_count,
        scratch_shapes=[pltpu.VMEM((act_total * BLK, HEAD_SIZE), jnp.bfloat16)] * 2
        + [pltpu.VMEM((act_total * BLK, HEAD_SIZE), jnp.float32)] * 2,
        input_output_aliases=aliases,
        compiler_params=pltpu.CompilerParams(vmem_limit_bytes=60 * 1024 * 1024),
        cost_estimate=lasting(2 if chunk == 1 else 9),
        name="attend",
    )(*operands)
    return outs[0], outs[1], outs[2:]


def token_kernel(tables, indices, rank_ref, *refs):
    out_ref = refs[-1]
    dkv_refs, refs = refs[: len(tables)], refs[len(tables) : -1]
    width = dkv_refs[0].shape[1] // 2
    count = len(tables[0])
    rows = out_ref.shape[-1] if len(out_ref.shape) == 3 else out_ref.shape[1] // count
    for at in range(count):
        owner = rank_ref[1] ^ at
        total = None
        for dkv_ref, table, index in zip(dkv_refs, tables, indices):
            arrays = [refs[number] for number in index]
            for side in range(2):
                term = dot(
                    dkv_ref[:, side * width : (side + 1) * width], side_of(table, arrays, at, side), 1, 1
                )
                total = term if total is None else total + term
        if len(out_ref.shape) == 3:
            out_ref[owner] = total.astype(out_ref.dtype)
        else:
            out_ref[:, pl.ds(pl.multiple_of(owner * rows, 128), rows)] = total.astype(out_ref.dtype)


def token_grads(rank, dkvs, weight_pieces, rows):
    flat, indices = [], []
    for arrays, _ in weight_pieces:
        index = []
        for array in arrays:
            known = [at for at, other in enumerate(flat) if other is array]
            if not known:
                known = [len(flat)]
                flat.append(array)
            index.append(known[0])
        indices.append(tuple(index))
    tables = tuple(table for _, table in weight_pieces)
    count = lax.axis_size("dp")
    tok_dev = dkvs[0].shape[0]
    flat_out = rows % 128 == 0
    shape = (tok_dev, count * rows) if flat_out else (count, tok_dev, rows)
    out = pl.pallas_call(
        functools.partial(token_kernel, tables, tuple(indices)),
        out_shape=jax.ShapeDtypeStruct(shape, jnp.bfloat16),
        in_specs=[smem()] + [vmem()] * (len(dkvs) + len(flat)),
        out_specs=vmem(),
        compiler_params=params(),
        cost_estimate=lasting(8),
        name="token_grads",
    )(rank, *dkvs, *flat)
    return out if flat_out else jnp.concatenate(list(out), axis=1)


def weight_kernel(dests, pieces_total, has_before, rank_ref, *refs):
    x_refs, refs = refs[:PARTS], refs[PARTS:]
    count = x_refs[0].shape[0]
    height = x_refs[0].shape[1] * PARTS
    pieces, refs = refs[:pieces_total], refs[pieces_total:]
    out_refs = refs[len(refs) // 2 :] if has_before else refs
    column, width = out_refs[0].shape[1], pieces[0].shape[1] // 2
    totals = [None, None]
    for at in range(count):
        rows = rows_of(x_refs, rank_ref[1] ^ at)
        for side in range(2):
            if pieces_total == count:
                piece, start = pieces[at], 0
            else:
                piece, start = pieces[at % 2], at // 2 * height
            term = dot(rows, piece[start : start + height, side * width : (side + 1) * width], 0, 0)
            totals[side] = term if totals[side] is None else totals[side] + term
    for at, out_ref in enumerate(out_refs):
        if has_before:
            out_ref[...] = refs[at][...]
        for dest, side, offset in dests:

            @pl.when(rank_ref[0] ^ at == dest)
            def _():
                out_ref[...] = totals[side][:, offset : offset + column].astype(out_ref.dtype)


def weight_terms(rank, x_all, pieces, dests, column, before):
    seq_count = lax.axis_size("seq")
    rows = x_all[0].shape[2]
    operands = [*x_all, *pieces, *before]
    return pl.pallas_call(
        functools.partial(weight_kernel, dests, len(pieces), bool(before)),
        out_shape=[jax.ShapeDtypeStruct((rows, column), jnp.float32)]
        + [jax.ShapeDtypeStruct((rows, column), jnp.bfloat16)] * (seq_count - 1),
        in_specs=[smem()] + [vmem()] * len(operands),
        out_specs=[vmem()] * seq_count,
        compiler_params=params(),
        cost_estimate=lasting(4),
        name="weight_grad",
    )(rank, *operands)


def body(tokens, queries, cotangent, kv_weight, active):
    seq_count, dp_count = lax.axis_size("seq"), lax.axis_size("dp")
    seq_rank, dp_rank = lax.axis_index("seq"), lax.axis_index("dp")
    tok_dev, model = tokens.shape[1], tokens.shape[2]
    qwidth, kvwidth = queries.shape[2], kv_weight.shape[1]
    rows = kv_weight.shape[0]
    act_total = active.shape[1]
    kv_heads = kvwidth // (2 * HEAD_SIZE)
    group = qwidth // (HEAD_SIZE * kv_heads)
    heads = kv_heads // CHUNKS
    width = heads * HEAD_SIZE
    blocks_dev = tok_dev // BLK
    column = kvwidth // seq_count

    block_ids = active[0]
    local_ids = seq_rank * blocks_dev + jnp.arange(blocks_dev, dtype=jnp.int32)
    match = (block_ids[None, :] == local_ids[:, None]).astype(jnp.int32)
    slot_rank = jnp.sum(match * jnp.arange(1, act_total + 1, dtype=jnp.int32)[None, :], axis=1) - 1
    info = jnp.concatenate(
        [seq_rank - block_ids // blocks_dev, block_ids % blocks_dev, slot_rank]
    ).astype(jnp.int32)
    rank = jnp.stack([seq_rank, dp_rank]).astype(jnp.int32)

    x_by_owner = split_columns(tokens, dp_count)

    dq = None
    dkvs, terms = [], []
    shards = []
    for chunk in range(CHUNKS):
        key_at, value_at = chunk * width, kvwidth // 2 + chunk * width
        shards.append(
            jnp.concatenate(
                [kv_weight[:, key_at : key_at + width], kv_weight[:, value_at : value_at + width]], axis=1
            )
        )
    weight_pieces, keyvals, weight_gates = gather_weights(
        shards, x_by_owner, lambda pieces: relay(project(rank, x_by_owner, pieces))
    )
    arrivals, keyvals = keyvals, [steps[0] for steps in keyvals]
    for chunk in range(1, CHUNKS):
        keyvals.append(project(rank, x_by_owner, weight_pieces[chunk]))
        arrivals[-1] = arrivals[-1] if chunk == 1 else finish(arrivals[-1], keyvals[-1])
        arrivals.append(spread(keyvals[-1]))
    arrivals = [steps[1:] for steps in [*arrivals[:-1], finish(arrivals[-1])]]
    x_all, gates = [], (keyvals[-1],)
    for part in x_by_owner:
        part = lax.all_to_all(after(part, *gates), "dp", split_axis=0, concat_axis=0, tiled=True)
        x_all.append(part)
        gates = (part,)

    backs, owns = [], []
    gates, waits, later = (keyvals[-1],), tuple(arrivals[-1][1:2]), ()
    for chunk in range(CHUNKS):
        kv_steps = [keyvals[chunk]] + arrivals[chunk]
        dq, own, sends = attend(
            after(info, *gates), queries, cotangent, kv_steps, chunk, heads, group, act_total, dq
        )
        if chunk < CHUNKS - 1 or seq_count > 4:
            arrived, back = collect(sends, waits, later)
        else:
            back = [moved(after(sends[step - 1], *waits), "seq", -step) for step in range(seq_count - 1, 0, -1)]
            arrived = ()
        backs.append(back)
        owns.append(own)
        gates, waits, later = tuple(arrived), (*back, *x_all), ()
    gates, sums = (owns[-1],), ()
    for chunk in range(CHUNKS):
        total = after(owns[chunk], *gates)
        for part in backs[chunk]:
            total = total + part.astype(jnp.float32)
        dkvs.append(total.astype(jnp.bfloat16))
        if chunk < CHUNKS - 1 or lax.axis_size("dp") > 8:
            dkv_pieces = gather_doubling(dkvs[chunk], backs[-1][:1], backs[-1][1:])
        else:
            dkv_pieces = gather_direct(dkvs[chunk], *sums[:1])
        dests = []
        for side in range(2):
            start = side * (kvwidth // 2) + chunk * width
            for offset in range(0, width, column):
                dests.append(((start + offset) // column, side, offset))
        sums = weight_terms(rank, x_all, dkv_pieces, dests, column, sums)
        gates = ()
    gates = (sums[0],)
    terms = [sums[0]]
    for mask in (*range(2, seq_count), 1):
        terms.append(exchange(sums[mask], "seq", mask).astype(jnp.float32))
    weight_grad = functools.reduce(lambda a, b: a + b, terms)
    token_grad = token_grads(after(rank, *gates), dkvs, weight_pieces, rows)
    return (dq, token_grad[None], weight_grad)


def solution(mesh):
    in_specs = (
        P("dp", "seq", None),
        P("dp", "seq", None),
        P("dp", "seq", None),
        P("dp", None),
        P("dp", None),
    )
    out_specs = (P("dp", "seq", None), P("dp", "seq", None), P("dp", "seq"))
    return jax.shard_map(body, mesh=mesh, in_specs=in_specs, out_specs=out_specs, check_vma=False)
```

```python
import functools
import math

import jax
import jax.numpy as jnp
from jax import lax
from jax.experimental import pallas as pl
from jax.experimental.pallas import tpu as pltpu
from jax.sharding import PartitionSpec as P

HEAD_SIZE = 128
BLK = 128
CHUNKS = 2
PARTS = 1
VMEM_BYTES = 24 * 1024 * 1024
MASKED = -1e30


def params():
    return pltpu.CompilerParams(vmem_limit_bytes=VMEM_BYTES)


def lasting(microseconds):
    return pl.CostEstimate(flops=4000000000 * microseconds, bytes_accessed=12000000 * microseconds, transcendentals=0)


def vmem():
    return pl.BlockSpec(memory_space=pltpu.VMEM)


def smem():
    return pl.BlockSpec(memory_space=pltpu.SMEM)


def dot(left, right, left_dim, right_dim):
    return lax.dot_general(
        left, right, (((left_dim,), (right_dim,)), ((), ())), preferred_element_type=jnp.float32
    )


def exchange(value, axis, mask):
    count = lax.axis_size(axis)
    return lax.ppermute(value, axis, [(i, i ^ mask) for i in range(count)])


def moved(value, axis, step, first=0):
    count = lax.axis_size(axis)
    pairs = [(i, i + step) for i in range(first, count) if 0 <= i + step < count]
    return lax.ppermute(value, axis, pairs)


def spread(value):
    count = lax.axis_size("seq")
    steps = [value] + [None] * (count - 1)
    for step in range(2, count, 2):
        steps[step] = moved(steps[step - 2], "seq", 2, step - 2)
    if count > 1:
        steps[1] = moved(value, "seq", 1)
    return steps


def relay(value):
    steps = [value]
    for step in range(1, lax.axis_size("seq")):
        steps.append(moved(steps[-1], "seq", 1, step - 1))
    return steps


def finish(steps, *gates):
    for step in range(3, len(steps), 2):
        steps[step] = moved(after(steps[step - 1], *gates), "seq", 1, step - 1)
    return steps


def added(left, right):
    return (left.astype(jnp.float32) + right.astype(jnp.float32)).astype(left.dtype)


def collect(sends, gates, later):
    count = lax.axis_size("seq")
    sends = [None, *sends]
    sends = [None] + [after(send, *gates) for send in sends[1:]]
    arrived = []
    for step in range(3, count, 2):
        arrived.append(moved(sends[step], "seq", -1, step))
        sends[step - 1] = added(sends[step - 1], arrived[-1])
    if len(sends) > 2:
        sends[2] = after(sends[2], *later)
    for step in range((count - 1) // 2 * 2, 2, -2):
        sends[step - 2] = added(sends[step - 2], moved(sends[step], "seq", -2, step))
    return arrived, [moved(sends[step], "seq", -step, step) for step in (1, 2) if step < count]


def gather_direct(own):
    count = lax.axis_size("dp")
    pieces = [own] + [None] * (count - 1)
    for mask in range(2, count, 2):
        pieces[mask] = exchange(own, "dp", mask)
    for mask in range(0, count, 2):
        pieces[mask + 1] = exchange(pieces[mask], "dp", 1)
    return pieces


def gather_doubling(own, second, last):
    bit, stack = 2, own
    while bit < lax.axis_size("dp"):
        stack = jnp.concatenate([stack, exchange(stack, "dp", bit)], axis=0)
        if bit == 2:
            stack = after(stack, *second)
        bit *= 2
    return [stack, exchange(after(stack, *last), "dp", 1)]


def after(value, *others):
    return lax.optimization_barrier((value, others))[0]


def side_of(table, refs, at, side):
    array, start, width = table[at][side]
    return refs[array][:, start : start + width]


def whole_table(count, width):
    return tuple(((at, 0, width), (at, width, width)) for at in range(count))


def halves_kernel(near_ref, far_ref, left_ref, right_ref, *, near_start, far_start):
    width = left_ref.shape[1]
    left_ref[...] = near_ref[:, near_start : near_start + width]
    right_ref[...] = far_ref[:, far_start : far_start + width]


def halves(near, far, near_start, far_start):
    shape = jax.ShapeDtypeStruct((near.shape[0], near.shape[1] // 2), near.dtype)
    return pl.pallas_call(
        functools.partial(halves_kernel, near_start=near_start, far_start=far_start),
        out_shape=[shape, shape],
        in_specs=[vmem()] * 2,
        out_specs=[vmem()] * 2,
        compiler_params=params(),
        cost_estimate=lasting(1),
        name="halves",
    )(near, far)


def gather_weights(shards, behind, use_first):
    count = lax.axis_size("dp")
    width = shards[0].shape[1] // 2
    if count != 8 or len(shards) != 2:
        result = []
        for shard in shards:
            pieces = gather_direct(shard)
            result.append((pieces, whole_table(count, width)))
        return result, [use_first(result[0])], pieces[-1:]
    first, second = shards
    table = []
    for entry in [((0, 0), (0, 1)), ((1, 0), (1, 1)), ((2, 0), (2, 1)), ((3, 0), (4, 0))]:
        for core in range(2):
            table.append(tuple((array + core * 5, part * width, width) for array, part in entry))
    table = tuple(table)

    def near_of(own, *gates):
        from_x, from_y = after((exchange(own, "dp", 2), exchange(own, "dp", 4)), *gates)
        to_y, to_x = halves(from_x, from_y, 0, width)
        return [from_x, from_y, exchange(to_y, "dp", 4), exchange(to_x, "dp", 2)]

    def with_core(own, own_core, others):
        cores = [exchange(part, "dp", 1) for part in others]
        return [own, *others, own_core, *cores], table

    others = near_of(first, *behind, second)
    pieces = [with_core(first, exchange(first, "dp", 1), others)]
    used = use_first(pieces[0])
    hops = list(used[1:]) + [used[0]] * 3
    second_core = exchange(after(second, used[0]), "dp", 1)
    others = near_of(after(second, *others[2:]), hops[0], second_core)
    pieces.append(with_core(second, second_core, [*others[:2], *after(tuple(others[2:]), hops[1])]))
    return pieces, [used], hops[1:2]


def split_kernel(x_ref, *out_refs):
    for at, out_ref in enumerate(out_refs):
        height = out_ref.shape[0]
        out_ref[...] = x_ref[at * height : (at + 1) * height]


def split_columns(tokens, count):
    tok_dev, model = tokens.shape[1:]
    rows, height = model // count, tok_dev // PARTS
    if rows % 128:
        return [
            jnp.stack([tokens[0, part * height : (part + 1) * height, at * rows : (at + 1) * rows] for at in range(count)])
            for part in range(PARTS)
        ]
    return pl.pallas_call(
        split_kernel,
        grid=(count,),
        out_shape=[jax.ShapeDtypeStruct((count, height, rows), tokens.dtype)] * PARTS,
        in_specs=[pl.BlockSpec((None, tok_dev, rows), lambda at: (0, 0, at))],
        out_specs=[pl.BlockSpec((None, height, rows), lambda at: (at, 0, 0))] * PARTS,
        compiler_params=params(),
        cost_estimate=lasting(3),
        name="split_columns",
    )(tokens)


def rows_of(x_refs, owner):
    return jnp.concatenate([x_ref[owner] for x_ref in x_refs], axis=0)


def project_kernel(table, rank_ref, *refs):
    x_refs, refs, out_ref = refs[:PARTS], refs[PARTS:-1], refs[-1]
    width = out_ref.shape[1] // 2
    totals = [None, None]
    for at in range(len(table)):
        rows = rows_of(x_refs, rank_ref[1] ^ at)
        for side in range(2):
            term = dot(rows, side_of(table, refs, at, side), 1, 0)
            totals[side] = term if totals[side] is None else totals[side] + term
    for side in range(2):
        out_ref[:, side * width : (side + 1) * width] = totals[side].astype(out_ref.dtype)


def project(rank, x_by_owner, pieces):
    arrays, table = pieces
    tok_dev, width = x_by_owner[0].shape[1] * PARTS, table[0][0][2] * 2
    return pl.pallas_call(
        functools.partial(project_kernel, table),
        out_shape=jax.ShapeDtypeStruct((tok_dev, width), jnp.bfloat16),
        in_specs=[smem()] + [vmem()] * (PARTS + len(arrays)),
        out_specs=vmem(),
        compiler_params=params(),
        cost_estimate=lasting(4),
        name="project",
    )(rank, *x_by_owner, *arrays)


def attend_kernel(sizes, info_ref, q_ref, g_ref, *refs):
    act_total, blocks_dev, seq_count, group, has_alias = sizes
    kv_refs = refs[: 2 * seq_count]
    refs = refs[2 * seq_count + (1 if has_alias else 0) :]
    dq_ref, own_ref = refs[0], refs[1]
    send_refs = refs[2 : 1 + seq_count]
    k_scr, v_scr, dk_scr, dv_scr = refs[1 + seq_count :]
    head = pl.program_id(0)
    width = own_ref.shape[1] // 2
    scale = 1.0 / math.sqrt(HEAD_SIZE)
    columns = [pl.ds(pl.multiple_of(side * width + head * HEAD_SIZE, HEAD_SIZE), HEAD_SIZE) for side in range(2)]
    dk_scr[...] = jnp.zeros_like(dk_scr)
    dv_scr[...] = jnp.zeros_like(dv_scr)
    for slot in range(act_total):
        steps = info_ref[slot]
        row = pl.multiple_of(info_ref[act_total + slot] * BLK, BLK)
        rows = slice(slot * BLK, (slot + 1) * BLK)

        @pl.when(steps < 0)
        def _():
            k_scr[rows, :] = jnp.zeros((BLK, HEAD_SIZE), k_scr.dtype)
            v_scr[rows, :] = jnp.zeros((BLK, HEAD_SIZE), v_scr.dtype)

        for step in range(seq_count):

            @pl.when(steps == step)
            def _():
                k_scr[rows, :] = kv_refs[2 * step][pl.ds(row, BLK), :]
                v_scr[rows, :] = kv_refs[2 * step + 1][pl.ds(row, BLK), :]

    def attend_block(rows, slots):
        span = slots * BLK
        keys, values = k_scr[:span, :], v_scr[:span, :]
        query, gradient = (
            jnp.concatenate([ref[rows, at * HEAD_SIZE : (at + 1) * HEAD_SIZE] for at in range(group)], axis=0)
            for ref in (q_ref, g_ref)
        )
        scores = dot(keys, query, 1, 1)
        last = scores[span - BLK :]
        key_pos = lax.broadcasted_iota(jnp.int32, last.shape, 0)
        query_pos = lax.broadcasted_iota(jnp.int32, last.shape, 1) & (BLK - 1)
        last = jnp.where(key_pos <= query_pos, last, MASKED)
        scores = last if slots == 1 else jnp.concatenate([scores[: span - BLK], last], axis=0)
        top = jnp.max(scores, axis=0, keepdims=True)
        exponent = jnp.exp2((scores - top) * (scale * math.log2(math.e)))
        probs = exponent * (1.0 / jnp.sum(exponent, axis=0, keepdims=True))
        dprobs = dot(values, gradient, 1, 1)
        delta = jnp.sum(probs * dprobs, axis=0, keepdims=True)
        dscores = (probs * (dprobs - delta)).astype(jnp.bfloat16)
        dk_scr[:span, :] += dot(dscores, query, 1, 0)
        dv_scr[:span, :] += dot(probs.astype(jnp.bfloat16), gradient, 1, 0)
        dquery = (dot(keys, dscores, 0, 0) * scale).T.astype(dq_ref.dtype)
        for at in range(group):
            dq_ref[rows, at * HEAD_SIZE : (at + 1) * HEAD_SIZE] = dquery[at * BLK : (at + 1) * BLK]

    @pl.loop(0, blocks_dev)
    def _(block):
        rank = info_ref[2 * act_total + block]
        rows = pl.ds(pl.multiple_of(block * BLK, BLK), BLK)

        @pl.when(rank < 0)
        def _():
            dq_ref[rows, :] = jnp.zeros((BLK, group * HEAD_SIZE), dq_ref.dtype)

        for slots in range(1, act_total + 1):

            @pl.when(rank == slots - 1)
            def _():
                attend_block(rows, slots)

    for target in (own_ref, *send_refs):
        for side in range(2):
            target[:, columns[side]] = jnp.zeros((target.shape[0], HEAD_SIZE), target.dtype)
    for slot in range(act_total):
        steps = info_ref[slot]
        row = pl.multiple_of(info_ref[act_total + slot] * BLK, BLK)
        rows = slice(slot * BLK, (slot + 1) * BLK)
        for step, target in enumerate((own_ref, *send_refs)):

            @pl.when(steps == step)
            def _():
                target[pl.ds(row, BLK), columns[0]] = (dk_scr[rows, :] * scale).astype(target.dtype)
                target[pl.ds(row, BLK), columns[1]] = dv_scr[rows, :].astype(target.dtype)


def attend(info, queries, cotangent, kv_steps, chunk, heads, group, act_total, dq_so_far):
    seq_count = len(kv_steps)
    tok_dev, width = kv_steps[0].shape
    qwidth = queries.shape[2]
    group_width = group * HEAD_SIZE
    q_spec = pl.BlockSpec((None, tok_dev, group_width), lambda i: (0, 0, chunk * heads + i))
    kv_specs = [
        pl.BlockSpec((tok_dev, HEAD_SIZE), lambda i: (0, i)),
        pl.BlockSpec((tok_dev, HEAD_SIZE), lambda i: (0, heads + i)),
    ]
    whole_spec = pl.BlockSpec((tok_dev, width), lambda i: (0, 0))
    sizes = (act_total, tok_dev // BLK, seq_count, group, dq_so_far is not None)
    operands = [info, queries, cotangent, *[kv for kv in kv_steps for _ in range(2)]]
    in_specs = [smem(), q_spec, q_spec] + kv_specs * seq_count
    aliases = {}
    if dq_so_far is not None:
        aliases = {len(operands): 0}
        operands.append(dq_so_far)
        in_specs.append(pl.BlockSpec(memory_space=pl.ANY))
    outs = pl.pallas_call(
        functools.partial(attend_kernel, sizes),
        grid=(heads,),
        out_shape=[
            jax.ShapeDtypeStruct((1, tok_dev, qwidth), jnp.bfloat16),
            jax.ShapeDtypeStruct((tok_dev, width), jnp.float32),
            *[jax.ShapeDtypeStruct((tok_dev, width), jnp.bfloat16) for _ in range(seq_count - 1)],
        ],
        in_specs=in_specs,
        out_specs=[q_spec] + [whole_spec] * seq_count,
        scratch_shapes=[pltpu.VMEM((act_total * BLK, HEAD_SIZE), jnp.bfloat16)] * 2
        + [pltpu.VMEM((act_total * BLK, HEAD_SIZE), jnp.float32)] * 2,
        input_output_aliases=aliases,
        compiler_params=pltpu.CompilerParams(vmem_limit_bytes=60 * 1024 * 1024),
        cost_estimate=lasting(2 if chunk == 1 else 9),
        name="attend",
    )(*operands)
    return outs[0], outs[1], outs[2:]


def token_kernel(tables, indices, rank_ref, *refs):
    out_ref = refs[-1]
    dkv_refs, refs = refs[: len(tables)], refs[len(tables) : -1]
    width = dkv_refs[0].shape[1] // 2
    count = len(tables[0])
    rows = out_ref.shape[-1] if len(out_ref.shape) == 3 else out_ref.shape[1] // count
    for at in range(count):
        owner = rank_ref[1] ^ at
        total = None
        for dkv_ref, table, index in zip(dkv_refs, tables, indices):
            arrays = [refs[number] for number in index]
            for side in range(2):
                term = dot(
                    dkv_ref[:, side * width : (side + 1) * width], side_of(table, arrays, at, side), 1, 1
                )
                total = term if total is None else total + term
        if len(out_ref.shape) == 3:
            out_ref[owner] = total.astype(out_ref.dtype)
        else:
            out_ref[:, pl.ds(pl.multiple_of(owner * rows, 128), rows)] = total.astype(out_ref.dtype)


def token_grads(rank, dkvs, weight_pieces, rows):
    flat, indices = [], []
    for arrays, _ in weight_pieces:
        index = []
        for array in arrays:
            known = [at for at, other in enumerate(flat) if other is array]
            if not known:
                known = [len(flat)]
                flat.append(array)
            index.append(known[0])
        indices.append(tuple(index))
    tables = tuple(table for _, table in weight_pieces)
    count = lax.axis_size("dp")
    tok_dev = dkvs[0].shape[0]
    flat_out = rows % 128 == 0
    shape = (tok_dev, count * rows) if flat_out else (count, tok_dev, rows)
    out = pl.pallas_call(
        functools.partial(token_kernel, tables, tuple(indices)),
        out_shape=jax.ShapeDtypeStruct(shape, jnp.bfloat16),
        in_specs=[smem()] + [vmem()] * (len(dkvs) + len(flat)),
        out_specs=vmem(),
        compiler_params=params(),
        cost_estimate=lasting(8),
        name="token_grads",
    )(rank, *dkvs, *flat)
    return out if flat_out else jnp.concatenate(list(out), axis=1)


def weight_kernel(dests, pieces_total, has_before, rank_ref, *refs):
    x_refs, refs = refs[:PARTS], refs[PARTS:]
    count = x_refs[0].shape[0]
    height = x_refs[0].shape[1] * PARTS
    pieces, refs = refs[:pieces_total], refs[pieces_total:]
    out_refs = refs[len(refs) // 2 :] if has_before else refs
    column, width = out_refs[0].shape[1], pieces[0].shape[1] // 2
    totals = [None, None]
    for at in range(count):
        rows = rows_of(x_refs, rank_ref[1] ^ at)
        for side in range(2):
            if pieces_total == count:
                piece, start = pieces[at], 0
            else:
                piece, start = pieces[at % 2], at // 2 * height
            term = dot(rows, piece[start : start + height, side * width : (side + 1) * width], 0, 0)
            totals[side] = term if totals[side] is None else totals[side] + term
    for at, out_ref in enumerate(out_refs):
        if has_before:
            out_ref[...] = refs[at][...]
        for dest, side, offset in dests:

            @pl.when(rank_ref[0] ^ at == dest)
            def _():
                out_ref[...] = totals[side][:, offset : offset + column].astype(out_ref.dtype)


def weight_terms(rank, x_all, pieces, dests, column, before):
    seq_count = lax.axis_size("seq")
    rows = x_all[0].shape[2]
    operands = [*x_all, *pieces, *before]
    return pl.pallas_call(
        functools.partial(weight_kernel, dests, len(pieces), bool(before)),
        out_shape=[jax.ShapeDtypeStruct((rows, column), jnp.float32)]
        + [jax.ShapeDtypeStruct((rows, column), jnp.bfloat16)] * (seq_count - 1),
        in_specs=[smem()] + [vmem()] * len(operands),
        out_specs=[vmem()] * seq_count,
        compiler_params=params(),
        cost_estimate=lasting(4),
        name="weight_grad",
    )(rank, *operands)


def body(tokens, queries, cotangent, kv_weight, active):
    seq_count, dp_count = lax.axis_size("seq"), lax.axis_size("dp")
    seq_rank, dp_rank = lax.axis_index("seq"), lax.axis_index("dp")
    tok_dev, model = tokens.shape[1], tokens.shape[2]
    qwidth, kvwidth = queries.shape[2], kv_weight.shape[1]
    rows = kv_weight.shape[0]
    act_total = active.shape[1]
    kv_heads = kvwidth // (2 * HEAD_SIZE)
    group = qwidth // (HEAD_SIZE * kv_heads)
    heads = kv_heads // CHUNKS
    width = heads * HEAD_SIZE
    blocks_dev = tok_dev // BLK
    column = kvwidth // seq_count

    block_ids = active[0]
    local_ids = seq_rank * blocks_dev + jnp.arange(blocks_dev, dtype=jnp.int32)
    match = (block_ids[None, :] == local_ids[:, None]).astype(jnp.int32)
    slot_rank = jnp.sum(match * jnp.arange(1, act_total + 1, dtype=jnp.int32)[None, :], axis=1) - 1
    info = jnp.concatenate(
        [seq_rank - block_ids // blocks_dev, block_ids % blocks_dev, slot_rank]
    ).astype(jnp.int32)
    rank = jnp.stack([seq_rank, dp_rank]).astype(jnp.int32)

    x_by_owner = split_columns(tokens, dp_count)

    dq = None
    dkvs, terms = [], []
    shards = []
    for chunk in range(CHUNKS):
        key_at, value_at = chunk * width, kvwidth // 2 + chunk * width
        shards.append(
            jnp.concatenate(
                [kv_weight[:, key_at : key_at + width], kv_weight[:, value_at : value_at + width]], axis=1
            )
        )
    weight_pieces, keyvals, weight_gates = gather_weights(
        shards, x_by_owner, lambda pieces: relay(project(rank, x_by_owner, pieces))
    )
    arrivals, keyvals = keyvals, [steps[0] for steps in keyvals]
    for chunk in range(1, CHUNKS):
        keyvals.append(project(rank, x_by_owner, weight_pieces[chunk]))
        arrivals[-1] = arrivals[-1] if chunk == 1 else finish(arrivals[-1], keyvals[-1])
        arrivals.append(spread(keyvals[-1]))
    arrivals = [steps[1:] for steps in [*arrivals[:-1], finish(arrivals[-1])]]
    x_all, gates = [], (keyvals[-1],)
    for part in x_by_owner:
        part = lax.all_to_all(after(part, *gates), "dp", split_axis=0, concat_axis=0, tiled=True)
        x_all.append(part)
        gates = (part,)

    backs, owns = [], []
    gates, waits, later = (keyvals[-1],), tuple(arrivals[-1][1:2]), ()
    for chunk in range(CHUNKS):
        kv_steps = [keyvals[chunk]] + arrivals[chunk]
        dq, own, sends = attend(
            after(info, *gates), queries, cotangent, kv_steps, chunk, heads, group, act_total, dq
        )
        arrived, back = collect(sends, waits, later)
        backs.append(back)
        owns.append(own)
        gates, waits, later = tuple(arrived), (*back, *x_all), ()
    gates, sums = (owns[-1],), ()
    for chunk in range(CHUNKS):
        total = after(owns[chunk], *gates)
        for part in backs[chunk]:
            total = total + part.astype(jnp.float32)
        dkvs.append(total.astype(jnp.bfloat16))
        if chunk < CHUNKS - 1 or lax.axis_size("dp") > 8:
            dkv_pieces = gather_doubling(dkvs[chunk], backs[-1][:1], backs[-1][1:])
        else:
            dkv_pieces = gather_direct(dkvs[chunk])
        dests = []
        for side in range(2):
            start = side * (kvwidth // 2) + chunk * width
            for offset in range(0, width, column):
                dests.append(((start + offset) // column, side, offset))
        sums = weight_terms(rank, x_all, dkv_pieces, dests, column, sums)
        gates = ()
    gates = (sums[0],)
    terms = [sums[0]]
    for mask in (*range(2, seq_count), 1):
        terms.append(exchange(sums[mask], "seq", mask).astype(jnp.float32))
    weight_grad = functools.reduce(lambda a, b: a + b, terms)
    token_grad = token_grads(after(rank, *gates), dkvs, weight_pieces, rows)
    return (dq, token_grad[None], weight_grad)


def solution(mesh):
    in_specs = (
        P("dp", "seq", None),
        P("dp", "seq", None),
        P("dp", "seq", None),
        P("dp", None),
        P("dp", None),
    )
    out_specs = (P("dp", "seq", None), P("dp", "seq", None), P("dp", "seq"))
    return jax.shard_map(body, mesh=mesh, in_specs=in_specs, out_specs=out_specs, check_vma=False)
```

```python
import functools
import math

import jax
import jax.numpy as jnp
from jax import lax
from jax.experimental import pallas as pl
from jax.experimental.pallas import tpu as pltpu
from jax.sharding import PartitionSpec as P

HEAD_SIZE = 128
BLK = 128
CHUNKS = 2
PARTS = 1
VMEM_BYTES = 24 * 1024 * 1024
MASKED = -1e30


def params():
    return pltpu.CompilerParams(vmem_limit_bytes=VMEM_BYTES)


def lasting(microseconds):
    return pl.CostEstimate(flops=4000000000 * microseconds, bytes_accessed=12000000 * microseconds, transcendentals=0)


def vmem():
    return pl.BlockSpec(memory_space=pltpu.VMEM)


def smem():
    return pl.BlockSpec(memory_space=pltpu.SMEM)


def dot(left, right, left_dim, right_dim):
    return lax.dot_general(
        left, right, (((left_dim,), (right_dim,)), ((), ())), preferred_element_type=jnp.float32
    )


def exchange(value, axis, mask):
    count = lax.axis_size(axis)
    return lax.ppermute(value, axis, [(i, i ^ mask) for i in range(count)])


def moved(value, axis, step, first=0):
    count = lax.axis_size(axis)
    pairs = [(i, i + step) for i in range(first, count) if 0 <= i + step < count]
    return lax.ppermute(value, axis, pairs)


def spread(value):
    count = lax.axis_size("seq")
    steps = [value] + [None] * (count - 1)
    for step in range(2, count, 2):
        steps[step] = moved(steps[step - 2], "seq", 2, step - 2)
    if count > 1:
        steps[1] = moved(value, "seq", 1)
    return steps


def relay(value):
    steps = [value]
    for step in range(1, lax.axis_size("seq")):
        steps.append(moved(steps[-1], "seq", 1, step - 1))
    return steps


def finish(steps, *gates):
    for step in range(3, len(steps), 2):
        steps[step] = moved(after(steps[step - 1], *gates), "seq", 1, step - 1)
    return steps


def added(left, right):
    return (left.astype(jnp.float32) + right.astype(jnp.float32)).astype(left.dtype)


def collect(sends, gates, later):
    count = lax.axis_size("seq")
    sends = [None, *sends]
    sends = [None] + [after(send, *gates) for send in sends[1:]]
    arrived = []
    for step in range(3, count, 2):
        arrived.append(moved(sends[step], "seq", -1, step))
        sends[step - 1] = added(sends[step - 1], arrived[-1])
    if len(sends) > 2:
        sends[2] = after(sends[2], *later)
    for step in range((count - 1) // 2 * 2, 2, -2):
        sends[step - 2] = added(sends[step - 2], moved(sends[step], "seq", -2, step))
    return arrived, [moved(sends[step], "seq", -step, step) for step in (1, 2) if step < count]


def gather_direct(own):
    count = lax.axis_size("dp")
    pieces = [own] + [None] * (count - 1)
    for mask in range(2, count, 2):
        pieces[mask] = exchange(own, "dp", mask)
    for mask in range(0, count, 2):
        pieces[mask + 1] = exchange(pieces[mask], "dp", 1)
    return pieces


def gather_doubling(own, second, last):
    bit, stack = 2, own
    while bit < lax.axis_size("dp"):
        stack = jnp.concatenate([stack, exchange(stack, "dp", bit)], axis=0)
        if bit == 2:
            stack = after(stack, *second)
        bit *= 2
    return [stack, exchange(after(stack, *last), "dp", 1)]


def after(value, *others):
    return lax.optimization_barrier((value, others))[0]


def side_of(table, refs, at, side):
    array, start, width = table[at][side]
    return refs[array][:, start : start + width]


def whole_table(count, width):
    return tuple(((at, 0, width), (at, width, width)) for at in range(count))


def halves_kernel(near_ref, far_ref, left_ref, right_ref, *, near_start, far_start):
    width = left_ref.shape[1]
    left_ref[...] = near_ref[:, near_start : near_start + width]
    right_ref[...] = far_ref[:, far_start : far_start + width]


def halves(near, far, near_start, far_start):
    shape = jax.ShapeDtypeStruct((near.shape[0], near.shape[1] // 2), near.dtype)
    return pl.pallas_call(
        functools.partial(halves_kernel, near_start=near_start, far_start=far_start),
        out_shape=[shape, shape],
        in_specs=[vmem()] * 2,
        out_specs=[vmem()] * 2,
        compiler_params=params(),
        cost_estimate=lasting(1),
        name="halves",
    )(near, far)


def gather_weights(shards, behind, use_first):
    count = lax.axis_size("dp")
    width = shards[0].shape[1] // 2
    if count != 8 or len(shards) != 2:
        result = []
        for shard in shards:
            pieces = gather_direct(shard)
            result.append((pieces, whole_table(count, width)))
        return result, [use_first(result[0])], pieces[-1:]
    first, second = shards
    table = []
    for entry in [((0, 0), (0, 1)), ((1, 0), (1, 1)), ((2, 0), (2, 1)), ((3, 0), (4, 0))]:
        for core in range(2):
            table.append(tuple((array + core * 5, part * width, width) for array, part in entry))
    table = tuple(table)

    def near_of(own, *gates):
        from_x, from_y = after((exchange(own, "dp", 2), exchange(own, "dp", 4)), *gates)
        to_y, to_x = halves(from_x, from_y, 0, width)
        return [from_x, from_y, exchange(to_y, "dp", 4), exchange(to_x, "dp", 2)]

    def with_core(own, own_core, others):
        cores = [exchange(part, "dp", 1) for part in others]
        return [own, *others, own_core, *cores], table

    others = near_of(first, *behind, second)
    pieces = [with_core(first, exchange(first, "dp", 1), others)]
    used = use_first(pieces[0])
    hops = list(used[1:]) + [used[0]] * 3
    second_core = exchange(after(second, used[0]), "dp", 1)
    others = near_of(after(second, *others[2:]), hops[0], second_core)
    pieces.append(with_core(second, second_core, [*others[:2], *after(tuple(others[2:]), hops[1])]))
    return pieces, [used], hops[1:2]


def split_kernel(x_ref, *out_refs):
    for at, out_ref in enumerate(out_refs):
        height = out_ref.shape[0]
        out_ref[...] = x_ref[at * height : (at + 1) * height]


def split_columns(tokens, count):
    tok_dev, model = tokens.shape[1:]
    rows, height = model // count, tok_dev // PARTS
    if rows % 128:
        return [
            jnp.stack([tokens[0, part * height : (part + 1) * height, at * rows : (at + 1) * rows] for at in range(count)])
            for part in range(PARTS)
        ]
    return pl.pallas_call(
        split_kernel,
        grid=(count,),
        out_shape=[jax.ShapeDtypeStruct((count, height, rows), tokens.dtype)] * PARTS,
        in_specs=[pl.BlockSpec((None, tok_dev, rows), lambda at: (0, 0, at))],
        out_specs=[pl.BlockSpec((None, height, rows), lambda at: (at, 0, 0))] * PARTS,
        compiler_params=params(),
        cost_estimate=lasting(3),
        name="split_columns",
    )(tokens)


def rows_of(x_refs, owner):
    return jnp.concatenate([x_ref[owner] for x_ref in x_refs], axis=0)


def project_kernel(table, rank_ref, *refs):
    x_refs, refs, out_ref = refs[:PARTS], refs[PARTS:-1], refs[-1]
    width = out_ref.shape[1] // 2
    totals = [None, None]
    for at in range(len(table)):
        rows = rows_of(x_refs, rank_ref[1] ^ at)
        for side in range(2):
            term = dot(rows, side_of(table, refs, at, side), 1, 0)
            totals[side] = term if totals[side] is None else totals[side] + term
    for side in range(2):
        out_ref[:, side * width : (side + 1) * width] = totals[side].astype(out_ref.dtype)


def project(rank, x_by_owner, pieces):
    arrays, table = pieces
    tok_dev, width = x_by_owner[0].shape[1] * PARTS, table[0][0][2] * 2
    return pl.pallas_call(
        functools.partial(project_kernel, table),
        out_shape=jax.ShapeDtypeStruct((tok_dev, width), jnp.bfloat16),
        in_specs=[smem()] + [vmem()] * (PARTS + len(arrays)),
        out_specs=vmem(),
        compiler_params=params(),
        cost_estimate=lasting(4),
        name="project",
    )(rank, *x_by_owner, *arrays)


def attend_kernel(sizes, info_ref, q_ref, g_ref, *refs):
    act_total, blocks_dev, seq_count, group, has_alias = sizes
    kv_refs = refs[: 2 * seq_count]
    refs = refs[2 * seq_count + (1 if has_alias else 0) :]
    dq_ref, own_ref = refs[0], refs[1]
    send_refs = refs[2 : 1 + seq_count]
    k_scr, v_scr, dk_scr, dv_scr = refs[1 + seq_count :]
    head = pl.program_id(0)
    width = own_ref.shape[1] // 2
    scale = 1.0 / math.sqrt(HEAD_SIZE)
    columns = [pl.ds(pl.multiple_of(side * width + head * HEAD_SIZE, HEAD_SIZE), HEAD_SIZE) for side in range(2)]
    dk_scr[...] = jnp.zeros_like(dk_scr)
    dv_scr[...] = jnp.zeros_like(dv_scr)
    for slot in range(act_total):
        steps = info_ref[slot]
        row = pl.multiple_of(info_ref[act_total + slot] * BLK, BLK)
        rows = slice(slot * BLK, (slot + 1) * BLK)

        @pl.when(steps < 0)
        def _():
            k_scr[rows, :] = jnp.zeros((BLK, HEAD_SIZE), k_scr.dtype)
            v_scr[rows, :] = jnp.zeros((BLK, HEAD_SIZE), v_scr.dtype)

        for step in range(seq_count):

            @pl.when(steps == step)
            def _():
                k_scr[rows, :] = kv_refs[2 * step][pl.ds(row, BLK), :]
                v_scr[rows, :] = kv_refs[2 * step + 1][pl.ds(row, BLK), :]

    def attend_block(rows, slots):
        span = slots * BLK
        keys, values = k_scr[:span, :], v_scr[:span, :]
        query, gradient = (
            jnp.concatenate([ref[rows, at * HEAD_SIZE : (at + 1) * HEAD_SIZE] for at in range(group)], axis=0)
            for ref in (q_ref, g_ref)
        )
        scores = dot(keys, query, 1, 1)
        last = scores[span - BLK :]
        key_pos = lax.broadcasted_iota(jnp.int32, last.shape, 0)
        query_pos = lax.broadcasted_iota(jnp.int32, last.shape, 1) & (BLK - 1)
        last = jnp.where(key_pos <= query_pos, last, MASKED)
        scores = last if slots == 1 else jnp.concatenate([scores[: span - BLK], last], axis=0)
        top = jnp.max(scores, axis=0, keepdims=True)
        exponent = jnp.exp2((scores - top) * (scale * math.log2(math.e)))
        probs = exponent * (1.0 / jnp.sum(exponent, axis=0, keepdims=True))
        dprobs = dot(values, gradient, 1, 1)
        delta = jnp.sum(probs * dprobs, axis=0, keepdims=True)
        dscores = (probs * (dprobs - delta)).astype(jnp.bfloat16)
        dk_scr[:span, :] += dot(dscores, query, 1, 0)
        dv_scr[:span, :] += dot(probs.astype(jnp.bfloat16), gradient, 1, 0)
        dquery = (dot(keys, dscores, 0, 0) * scale).T.astype(dq_ref.dtype)
        for at in range(group):
            dq_ref[rows, at * HEAD_SIZE : (at + 1) * HEAD_SIZE] = dquery[at * BLK : (at + 1) * BLK]

    @pl.loop(0, blocks_dev)
    def _(block):
        rank = info_ref[2 * act_total + block]
        rows = pl.ds(pl.multiple_of(block * BLK, BLK), BLK)

        @pl.when(rank < 0)
        def _():
            dq_ref[rows, :] = jnp.zeros((BLK, group * HEAD_SIZE), dq_ref.dtype)

        for slots in range(1, act_total + 1):

            @pl.when(rank == slots - 1)
            def _():
                attend_block(rows, slots)

    for target in (own_ref, *send_refs):
        for side in range(2):
            target[:, columns[side]] = jnp.zeros((target.shape[0], HEAD_SIZE), target.dtype)
    for slot in range(act_total):
        steps = info_ref[slot]
        row = pl.multiple_of(info_ref[act_total + slot] * BLK, BLK)
        rows = slice(slot * BLK, (slot + 1) * BLK)
        for step, target in enumerate((own_ref, *send_refs)):

            @pl.when(steps == step)
            def _():
                target[pl.ds(row, BLK), columns[0]] = (dk_scr[rows, :] * scale).astype(target.dtype)
                target[pl.ds(row, BLK), columns[1]] = dv_scr[rows, :].astype(target.dtype)


def attend(info, queries, cotangent, kv_steps, chunk, heads, group, act_total, dq_so_far):
    seq_count = len(kv_steps)
    tok_dev, width = kv_steps[0].shape
    qwidth = queries.shape[2]
    group_width = group * HEAD_SIZE
    q_spec = pl.BlockSpec((None, tok_dev, group_width), lambda i: (0, 0, chunk * heads + i))
    kv_specs = [
        pl.BlockSpec((tok_dev, HEAD_SIZE), lambda i: (0, i)),
        pl.BlockSpec((tok_dev, HEAD_SIZE), lambda i: (0, heads + i)),
    ]
    whole_spec = pl.BlockSpec((tok_dev, width), lambda i: (0, 0))
    sizes = (act_total, tok_dev // BLK, seq_count, group, dq_so_far is not None)
    operands = [info, queries, cotangent, *[kv for kv in kv_steps for _ in range(2)]]
    in_specs = [smem(), q_spec, q_spec] + kv_specs * seq_count
    aliases = {}
    if dq_so_far is not None:
        aliases = {len(operands): 0}
        operands.append(dq_so_far)
        in_specs.append(pl.BlockSpec(memory_space=pl.ANY))
    outs = pl.pallas_call(
        functools.partial(attend_kernel, sizes),
        grid=(heads,),
        out_shape=[
            jax.ShapeDtypeStruct((1, tok_dev, qwidth), jnp.bfloat16),
            jax.ShapeDtypeStruct((tok_dev, width), jnp.float32),
            *[jax.ShapeDtypeStruct((tok_dev, width), jnp.bfloat16) for _ in range(seq_count - 1)],
        ],
        in_specs=in_specs,
        out_specs=[q_spec] + [whole_spec] * seq_count,
        scratch_shapes=[pltpu.VMEM((act_total * BLK, HEAD_SIZE), jnp.bfloat16)] * 2
        + [pltpu.VMEM((act_total * BLK, HEAD_SIZE), jnp.float32)] * 2,
        input_output_aliases=aliases,
        compiler_params=pltpu.CompilerParams(vmem_limit_bytes=60 * 1024 * 1024),
        cost_estimate=lasting(2 if chunk == 1 else 9),
        name="attend",
    )(*operands)
    return outs[0], outs[1], outs[2:]


def token_kernel(tables, indices, rank_ref, *refs):
    out_ref = refs[-1]
    dkv_refs, refs = refs[: len(tables)], refs[len(tables) : -1]
    width = dkv_refs[0].shape[1] // 2
    count = len(tables[0])
    rows = out_ref.shape[-1] if len(out_ref.shape) == 3 else out_ref.shape[1] // count
    for at in range(count):
        owner = rank_ref[1] ^ at
        total = None
        for dkv_ref, table, index in zip(dkv_refs, tables, indices):
            arrays = [refs[number] for number in index]
            for side in range(2):
                term = dot(
                    dkv_ref[:, side * width : (side + 1) * width], side_of(table, arrays, at, side), 1, 1
                )
                total = term if total is None else total + term
        if len(out_ref.shape) == 3:
            out_ref[owner] = total.astype(out_ref.dtype)
        else:
            out_ref[:, pl.ds(pl.multiple_of(owner * rows, 128), rows)] = total.astype(out_ref.dtype)


def token_grads(rank, dkvs, weight_pieces, rows):
    flat, indices = [], []
    for arrays, _ in weight_pieces:
        index = []
        for array in arrays:
            known = [at for at, other in enumerate(flat) if other is array]
            if not known:
                known = [len(flat)]
                flat.append(array)
            index.append(known[0])
        indices.append(tuple(index))
    tables = tuple(table for _, table in weight_pieces)
    count = lax.axis_size("dp")
    tok_dev = dkvs[0].shape[0]
    flat_out = rows % 128 == 0
    shape = (tok_dev, count * rows) if flat_out else (count, tok_dev, rows)
    out = pl.pallas_call(
        functools.partial(token_kernel, tables, tuple(indices)),
        out_shape=jax.ShapeDtypeStruct(shape, jnp.bfloat16),
        in_specs=[smem()] + [vmem()] * (len(dkvs) + len(flat)),
        out_specs=vmem(),
        compiler_params=params(),
        cost_estimate=lasting(8),
        name="token_grads",
    )(rank, *dkvs, *flat)
    return out if flat_out else jnp.concatenate(list(out), axis=1)


def weight_kernel(dests, pieces_total, has_before, rank_ref, *refs):
    x_refs, refs = refs[:PARTS], refs[PARTS:]
    count = x_refs[0].shape[0]
    height = x_refs[0].shape[1] * PARTS
    pieces, refs = refs[:pieces_total], refs[pieces_total:]
    out_refs = refs[len(refs) // 2 :] if has_before else refs
    column, width = out_refs[0].shape[1], pieces[0].shape[1] // 2
    totals = [None, None]
    for at in range(count):
        rows = rows_of(x_refs, rank_ref[1] ^ at)
        for side in range(2):
            if pieces_total == count:
                piece, start = pieces[at], 0
            else:
                piece, start = pieces[at % 2], at // 2 * height
            term = dot(rows, piece[start : start + height, side * width : (side + 1) * width], 0, 0)
            totals[side] = term if totals[side] is None else totals[side] + term
    for at, out_ref in enumerate(out_refs):
        if has_before:
            out_ref[...] = refs[at][...]
        for dest, side, offset in dests:

            @pl.when(rank_ref[0] ^ at == dest)
            def _():
                out_ref[...] = totals[side][:, offset : offset + column].astype(out_ref.dtype)


def weight_terms(rank, x_all, pieces, dests, column, before):
    seq_count = lax.axis_size("seq")
    rows = x_all[0].shape[2]
    operands = [*x_all, *pieces, *before]
    return pl.pallas_call(
        functools.partial(weight_kernel, dests, len(pieces), bool(before)),
        out_shape=[jax.ShapeDtypeStruct((rows, column), jnp.float32)]
        + [jax.ShapeDtypeStruct((rows, column), jnp.bfloat16)] * (seq_count - 1),
        in_specs=[smem()] + [vmem()] * len(operands),
        out_specs=[vmem()] * seq_count,
        compiler_params=params(),
        cost_estimate=lasting(4),
        name="weight_grad",
    )(rank, *operands)


def body(tokens, queries, cotangent, kv_weight, active):
    seq_count, dp_count = lax.axis_size("seq"), lax.axis_size("dp")
    seq_rank, dp_rank = lax.axis_index("seq"), lax.axis_index("dp")
    tok_dev, model = tokens.shape[1], tokens.shape[2]
    qwidth, kvwidth = queries.shape[2], kv_weight.shape[1]
    rows = kv_weight.shape[0]
    act_total = active.shape[1]
    kv_heads = kvwidth // (2 * HEAD_SIZE)
    group = qwidth // (HEAD_SIZE * kv_heads)
    heads = kv_heads // CHUNKS
    width = heads * HEAD_SIZE
    blocks_dev = tok_dev // BLK
    column = kvwidth // seq_count

    block_ids = active[0]
    local_ids = seq_rank * blocks_dev + jnp.arange(blocks_dev, dtype=jnp.int32)
    match = (block_ids[None, :] == local_ids[:, None]).astype(jnp.int32)
    slot_rank = jnp.sum(match * jnp.arange(1, act_total + 1, dtype=jnp.int32)[None, :], axis=1) - 1
    info = jnp.concatenate(
        [seq_rank - block_ids // blocks_dev, block_ids % blocks_dev, slot_rank]
    ).astype(jnp.int32)
    rank = jnp.stack([seq_rank, dp_rank]).astype(jnp.int32)

    x_by_owner = split_columns(tokens, dp_count)

    dq = None
    dkvs, terms = [], []
    shards = []
    for chunk in range(CHUNKS):
        key_at, value_at = chunk * width, kvwidth // 2 + chunk * width
        shards.append(
            jnp.concatenate(
                [kv_weight[:, key_at : key_at + width], kv_weight[:, value_at : value_at + width]], axis=1
            )
        )
    weight_pieces, keyvals, weight_gates = gather_weights(
        shards, x_by_owner, lambda pieces: relay(project(rank, x_by_owner, pieces))
    )
    arrivals, keyvals = keyvals, [steps[0] for steps in keyvals]
    for chunk in range(1, CHUNKS):
        keyvals.append(project(rank, x_by_owner, weight_pieces[chunk]))
        arrivals[-1] = arrivals[-1] if chunk == 1 else finish(arrivals[-1], keyvals[-1])
        arrivals.append(spread(keyvals[-1]))
    arrivals = [steps[1:] for steps in [*arrivals[:-1], finish(arrivals[-1])]]
    x_all, gates = [], (keyvals[-1],)
    for part in x_by_owner:
        part = lax.all_to_all(after(part, *gates), "dp", split_axis=0, concat_axis=0, tiled=True)
        x_all.append(part)
        gates = (part,)

    backs, owns = [], []
    gates, waits, later = (keyvals[-1],), tuple(arrivals[-1][1:2]), ()
    for chunk in range(CHUNKS):
        kv_steps = [keyvals[chunk]] + arrivals[chunk]
        dq, own, sends = attend(
            after(info, *gates), queries, cotangent, kv_steps, chunk, heads, group, act_total, dq
        )
        arrived, back = collect(sends, waits, later)
        backs.append(back)
        owns.append(own)
        gates, waits, later = tuple(arrived), (*back, *x_all), ()
    gates, sums = (owns[-1],), ()
    for chunk in range(CHUNKS):
        total = after(owns[chunk], *gates)
        for part in backs[chunk]:
            total = total + part.astype(jnp.float32)
        dkvs.append(total.astype(jnp.bfloat16))
        if chunk < CHUNKS - 1 or lax.axis_size("dp") > 8:
            dkv_pieces = gather_doubling(dkvs[chunk], backs[-1][:1], backs[-1][1:])
        else:
            dkv_pieces = gather_direct(dkvs[chunk])
        dests = []
        for side in range(2):
            start = side * (kvwidth // 2) + chunk * width
            for offset in range(0, width, column):
                dests.append(((start + offset) // column, side, offset))
        sums = weight_terms(rank, x_all, dkv_pieces, dests, column, sums)
        gates = ()
    gates = (sums[0],)
    terms = [sums[0]]
    for mask in (2, 1, *range(3, seq_count)):
        terms.append(exchange(sums[mask], "seq", mask).astype(jnp.float32))
    weight_grad = functools.reduce(lambda a, b: a + b, terms)
    token_grad = token_grads(after(rank, *gates), dkvs, weight_pieces, rows)
    return (dq, token_grad[None], weight_grad)


def solution(mesh):
    in_specs = (
        P("dp", "seq", None),
        P("dp", "seq", None),
        P("dp", "seq", None),
        P("dp", None),
        P("dp", None),
    )
    out_specs = (P("dp", "seq", None), P("dp", "seq", None), P("dp", "seq"))
    return jax.shard_map(body, mesh=mesh, in_specs=in_specs, out_specs=out_specs, check_vma=False)
```
